128 devices in a mesh: dp: 2 (over y_hi), row: 4 (over x), colxdept: 16 (over z, y_lo, core).
Axes of the slice: x: 4, y: 4 (y_hi: 2, y_lo: 2; y = y_hi * 2 + y_lo), z: 4, core: 2. Of those that a mesh axis runs over, the one named last changes fastest.
Arguments:
- tokens: bfloat16 [2, 512, 12288], P('dp', 'colxdept', 'row'), may hold values from -30 to 30
- w_qkv: bfloat16 [3, 12288, 6144], P(None, 'row', 'colxdept'), may hold values from -0.0546875 to 0.0546875
- w_out: bfloat16 [6144, 12288], P('colxdept', 'row'), may hold values from -0.078125 to 0.078125
- cotangent: bfloat16 [2, 512, 12288], P('dp', 'colxdept', 'row'), may hold values from -6 to 6
Outputs:
- mixed: bfloat16 [2, 512, 12288], P('dp', 'colxdept', 'row')
- grad_tokens: bfloat16 [2, 512, 12288], P('dp', 'colxdept', 'row')
- grad_qkv: bfloat16 [3, 12288, 6144], P(None, 'row', 'colxdept')
- grad_out: bfloat16 [6144, 12288], P('colxdept', 'row')
The draws below stay inside these ranges and needn't reach their ends.
All inputs are finite; a program needn't handle non-finite values.
Results may differ from the reference program's by a relative error of at most 0.02.
The reference program's roundings to bfloat16 on the way count: a program that leaves them out, or rounds other values in their place, can miss the bound.
Values may be sent and summed in bfloat16 or wider, within the bound.
No kernel may reach another device: no remote copies, remote signals or barrier semaphores. Data moves between devices by JAX's collectives and lax.ppermute only.
A program may use at most 128 MiB of HBM per device.

```python
import jax
import jax.numpy as jnp

D = 12288
HEADS = 48
DH = 128
SEQ = 512
N_DP = 2


def draw_tokens(key, part):
    key = jax.random.fold_in(key, 7)
    first = jax.random.fold_in(key, 0)
    base = jax.random.normal(first, (N_DP, SEQ, D), jnp.float32)
    values = jnp.clip(base, -6.0, 6.0)
    return values.astype(jnp.bfloat16)


def level_of(key, shape, pieces, smallest, top_value):
    gain, own = 1.0, jax.random.fold_in(key, 6)
    for axis_at, shards_of in pieces:
        steps = jnp.exp(jax.random.uniform(jax.random.fold_in(own, axis_at), (shards_of,), jnp.float32, smallest / len(pieces), top_value / len(pieces)))
        gain = gain * jnp.repeat(steps, shape[axis_at] // shards_of).reshape([-1 if axis == axis_at else 1 for axis in range(len(shape))])
    return gain


def bell_draw(own_key, shape, deviation, most, cuts=(), held_as=jnp.bfloat16):
    values = deviation * jax.random.normal(own_key, shape, jnp.float32)
    if cuts:
        values = values * level_of(own_key, shape, cuts, -0.22, 0.18)
    return jnp.clip(values, -most, most).astype(held_as)


def setup_inputs(seed: int = 0) -> dict:
    key_list = jax.random.split(jax.random.key(seed), 5)
    tokens = draw_tokens(jax.random.fold_in(key_list[4], 71), 0)
    w_qkv = bell_draw(key_list[1], (3, D, HEADS * DH), D ** -0.5, 0.0546875, ((1, 4), (2, 16)))
    w_out = bell_draw(key_list[2], (HEADS * DH, D), (HEADS * DH) ** -0.5, 0.078125, ((0, 16), (1, 4)))
    cotangent = bell_draw(key_list[3], (N_DP, SEQ, D), 1.0, 6.0, ((0, 2), (1, 16), (2, 4)))
    return dict(tokens=tokens, w_qkv=w_qkv, w_out=w_out, cotangent=cotangent)


def soft_rows(scores):
    top = jnp.max(scores, axis=-1, keepdims=True)
    expo = jnp.exp(scores - top)
    return expo / jnp.sum(expo, axis=-1, keepdims=True)


def reference(tokens, w_qkv, w_out, cotangent):
    batch = tokens.shape[0]
    width = HEADS * DH
    scale = 1.0 / (DH ** 0.5)
    flat = tokens.reshape(batch * SEQ, D)
    projs = [jnp.dot(flat, w_qkv[a], preferred_element_type=jnp.float32).astype(jnp.bfloat16) for a in range(3)]
    query, keys, values = [p.reshape(batch, SEQ, HEADS, DH).astype(jnp.float32) for p in projs]
    scores = jnp.einsum('bqhd,bkhd->bhqk', query, keys) * scale
    causal = jnp.arange(SEQ)[:, None] >= jnp.arange(SEQ)[None, :]
    scores = jnp.where(causal, scores, -1e30)
    probs = soft_rows(scores)
    probs_b = probs.astype(jnp.bfloat16).astype(jnp.float32)
    context = jnp.einsum('bhqk,bkhd->bqhd', probs_b, values).astype(jnp.bfloat16).reshape(batch * SEQ, width)
    mixed = jnp.dot(context, w_out, preferred_element_type=jnp.float32).astype(jnp.bfloat16)
    grads = cotangent.reshape(batch * SEQ, D)
    grad_out = jnp.dot(context.T, grads, preferred_element_type=jnp.float32).astype(jnp.bfloat16)
    grad_context = jnp.dot(grads, w_out.T, preferred_element_type=jnp.float32).astype(jnp.bfloat16)
    grad_ctx = grad_context.reshape(batch, SEQ, HEADS, DH).astype(jnp.float32)
    grad_probs = jnp.einsum('bqhd,bkhd->bhqk', grad_ctx, values)
    grad_value = jnp.einsum('bhqk,bqhd->bkhd', probs_b, grad_ctx).astype(jnp.bfloat16)
    delta = jnp.sum(grad_probs * probs, axis=-1, keepdims=True)
    grad_scores = (probs * (grad_probs - delta) * scale).astype(jnp.bfloat16).astype(jnp.float32)
    grad_query = jnp.einsum('bhqk,bkhd->bqhd', grad_scores, keys).astype(jnp.bfloat16)
    grad_key = jnp.einsum('bhqk,bqhd->bkhd', grad_scores, query).astype(jnp.bfloat16)
    grad_proj = [g.reshape(batch * SEQ, width) for g in (grad_query, grad_key, grad_value)]
    grad_qkv = jnp.stack([jnp.dot(flat.T, g, preferred_element_type=jnp.float32) for g in grad_proj]).astype(jnp.bfloat16)
    total = jnp.zeros((batch * SEQ, D), jnp.float32)
    for a in range(3):
        total = total + jnp.dot(grad_proj[a], w_qkv[a].T, preferred_element_type=jnp.float32)
    grad_tokens = total.astype(jnp.bfloat16)
    return (mixed.reshape(batch, SEQ, D), grad_tokens.reshape(batch, SEQ, D), grad_qkv, grad_out)
```

```python
import jax
import jax.numpy as jnp
from jax import lax
from jax.experimental import pallas as pl
from jax.experimental.pallas import tpu as pltpu
from jax.sharding import PartitionSpec as P

DH = 128
F32 = jnp.float32
BF16 = jnp.bfloat16
NT = (((1,), (1,)), ((), ()))
TN = (((0,), (0,)), ((), ()))


def dot(a, b, dims=None):
    if dims is None:
        return jnp.dot(a, b, preferred_element_type=F32)
    return lax.dot_general(a, b, dims, preferred_element_type=F32)


def soft_rows(q, k, rows, cols):
    scores = dot(q, k, NT) * (1.0 / DH**0.5)
    scores = jnp.where(rows >= cols, scores, -1e30)
    expo = jnp.exp(scores - jnp.max(scores, axis=-1, keepdims=True))
    return expo / jnp.sum(expo, axis=-1, keepdims=True)


def forward_kernel(rows, cols, q, k, v, context):
    probs = soft_rows(q[...], k[...], rows[...], cols[...])
    context[...] = dot(probs.astype(BF16), v[...]).astype(BF16)


def backward_kernel(rows, cols, q, k, v, g, gq, gk, gv):
    scale = 1.0 / DH**0.5
    probs = soft_rows(q[...], k[...], rows[...], cols[...])
    gv[...] = dot(probs.astype(BF16), g[...], TN).astype(BF16)
    grad_probs = dot(g[...], v[...], NT)
    delta = jnp.sum(grad_probs * probs, axis=-1, keepdims=True)
    grad_scores = (probs * (grad_probs - delta) * scale).astype(BF16)
    gq[...] = dot(grad_scores, k[...]).astype(BF16)
    gk[...] = dot(grad_scores, q[...], TN).astype(BF16)


def head_spec(seq, first):
    return pl.BlockSpec((seq, DH), lambda h: (0, first + h))


def attention(rows, cols, qkv, grad_context=None):
    seq, width = qkv.shape[0], qkv.shape[1] // 3
    heads = width // DH
    whole = [pl.BlockSpec((seq, 1), lambda h: (0, 0)), pl.BlockSpec((1, seq), lambda h: (0, 0))]
    ins = whole + [head_spec(seq, a * heads) for a in range(3)]
    args = [rows, cols, qkv, qkv, qkv]
    forward = grad_context is None
    n_out = 1 if forward else 3
    if not forward:
        ins.append(head_spec(seq, 0))
        args.append(grad_context)
    shape = jax.ShapeDtypeStruct((seq, width), BF16)
    return pl.pallas_call(
        forward_kernel if forward else backward_kernel,
        grid=(heads,),
        in_specs=ins,
        out_specs=[head_spec(seq, 0)] * n_out,
        out_shape=[shape] * n_out,
        compiler_params=pltpu.CompilerParams(vmem_limit_bytes=48 * 2**20),
        cost_estimate=pl.CostEstimate(
            flops=(2 if forward else 5) * 2 * heads * seq * seq * DH,
            bytes_accessed=(4 if forward else 7) * seq * width * 2,
            transcendentals=heads * seq * seq,
        ),
    )(*args)


def after(x, *others):
    return lax.optimization_barrier((x, *others))[0]


def body(tokens, w_qkv, w_out, cotangent):
    width = w_qkv.shape[2]
    n_row = lax.axis_size("row")
    n_col = lax.axis_size("colxdept")
    n_dp = lax.axis_size("dp")
    chips = n_col // 2
    tile = tokens.shape[1]
    seq = tile * n_col
    half, local = seq // 2, seq // n_row
    core = lax.axis_index("colxdept") % 2
    row = lax.axis_index("row")
    same_core = [list(range(c, n_col, 2)) for c in range(2)]

    def swap_cores(x):
        return lax.ppermute(x, "colxdept", [(i, i ^ 1) for i in range(n_col)])

    def swap_dp(x):
        return lax.ppermute(x, "dp", [(i, (i + 1) % n_dp) for i in range(n_dp)])

    def among_chips(x):
        return lax.all_to_all(x, "colxdept", 0, 0, axis_index_groups=same_core)

    def gather_core(x):
        return among_chips(jnp.broadcast_to(x[None], (chips, *x.shape)))

    def gather_row(x):
        shared = lax.all_to_all(jnp.broadcast_to(x[None], (n_row, *x.shape)), "row", 0, 0)
        return shared.reshape(n_row * x.shape[0], *x.shape[1:])

    def sum_row(x):
        parts = lax.all_to_all(x.reshape(n_row, local, x.shape[1]), "row", 0, 0)
        return jnp.sum(parts, axis=0)

    place = jnp.arange(seq, dtype=jnp.int32)
    owner = (place // half + core) % 2
    position = ((place % half) // tile * 2 + owner) * tile + place % tile
    rows, cols = position[:, None], position[None, :]

    tok_mine = gather_core(tokens[0]).reshape(half, -1)
    tok_sib = swap_cores(tok_mine)
    cot_mine = gather_core(after(cotangent[0], tok_mine)).reshape(half, -1)
    cot_sib = swap_cores(cot_mine)
    w_out_sib = swap_cores(after(w_out, tok_sib))
    w_qkv_sib = swap_cores(after(w_qkv, cot_sib))

    def project(x):
        return jnp.concatenate([dot(x, w_qkv[a]) for a in range(3)], axis=1)

    qkv_part = jnp.concatenate([project(tok_mine), project(tok_sib)], axis=0)
    qkv = gather_row(sum_row(qkv_part).astype(BF16))
    ctx_part = jnp.concatenate([dot(cot_mine, w_out, NT), dot(cot_sib, w_out, NT)], axis=0)
    grad_context = gather_row(sum_row(after(ctx_part, qkv_part)).astype(BF16))

    other = swap_dp(jnp.concatenate([after(tokens[0], cot_mine), cotangent[0]], axis=1))
    other_mine = lax.all_gather(other, "colxdept", axis=0, tiled=True, axis_index_groups=same_core)
    other_sib = swap_cores(other_mine)

    def split_other(x):
        return x[:, : x.shape[1] // 2], x[:, x.shape[1] // 2 :]

    (tok2_mine, cot2_mine), (tok2_sib, cot2_sib) = split_other(other_mine), split_other(other_sib)

    def from_other(x):
        return gather_row(swap_dp(lax.dynamic_slice_in_dim(x, row * local, local, axis=0)))

    def finish(part):
        parts = among_chips(part.astype(BF16).reshape(chips, tile, -1))
        return jnp.sum(parts.astype(F32), axis=0).astype(BF16)

    (context,) = attention(rows, cols, qkv)
    context_sib = swap_cores(context[half:])
    mixed = finish(dot(context[:half], w_out) + dot(context_sib, w_out_sib))
    context2 = from_other(context)
    grad_out = (
        dot(context[:half], cot_mine, TN)
        + dot(context[half:], cot_sib, TN)
        + dot(context2[:half], cot2_mine, TN)
        + dot(context2[half:], cot2_sib, TN)
    ).astype(BF16)

    grad_parts = attention(rows, cols, qkv, grad_context)
    grad_proj = jnp.concatenate(grad_parts, axis=1)
    grad_sib = swap_cores(grad_proj[half:])
    grad_proj2 = from_other(grad_proj)

    def piece(x, a):
        return x[:, a * width : (a + 1) * width]

    total = sum(
        dot(piece(grad_proj[:half], a), w_qkv[a], NT) + dot(piece(grad_sib, a), w_qkv_sib[a], NT)
        for a in range(3)
    )
    grad_tokens = finish(total)
    grad_qkv = jnp.stack(
        [
            (
                dot(tok_mine, piece(grad_proj[:half], a), TN)
                + dot(tok_sib, piece(grad_proj[half:], a), TN)
                + dot(tok2_mine, piece(grad_proj2[:half], a), TN)
                + dot(tok2_sib, piece(grad_proj2[half:], a), TN)
            ).astype(BF16)
            for a in range(3)
        ]
    )
    return (mixed[None], grad_tokens[None], grad_qkv, grad_out)


def solution(mesh):
    return jax.shard_map(
        body,
        mesh=mesh,
        in_specs=(
            P("dp", "colxdept", "row"),
            P(None, "row", "colxdept"),
            P("colxdept", "row"),
            P("dp", "colxdept", "row"),
        ),
        out_specs=(
            P("dp", "colxdept", "row"),
            P("dp", "colxdept", "row"),
            P(None, "row", "colxdept"),
            P("colxdept", "row"),
        ),
        check_vma=False,
    )
```

```python
import jax
import jax.numpy as jnp
from jax import lax
from jax.experimental import pallas as pl
from jax.experimental.pallas import tpu as pltpu
from jax.sharding import PartitionSpec as P

DH = 128
F32 = jnp.float32
BF16 = jnp.bfloat16
NT = (((1,), (1,)), ((), ()))
TN = (((0,), (0,)), ((), ()))
WIDE = 512


def dot(a, b, dims=None):
    if dims is None:
        return jnp.dot(a, b, preferred_element_type=F32)
    return lax.dot_general(a, b, dims, preferred_element_type=F32)


def call(kernel, grid, in_specs, out_specs, out_shape, flops, scratch=()):
    def run(*args):
        many = out_shape if isinstance(out_shape, list) else [out_shape]
        moved = sum(a.size * a.dtype.itemsize for a in [*args, *many])
        return pl.pallas_call(
            kernel,
            grid=grid,
            in_specs=in_specs,
            out_specs=out_specs,
            out_shape=out_shape,
            scratch_shapes=list(scratch),
            compiler_params=pltpu.CompilerParams(vmem_limit_bytes=48 * 2**20),
            cost_estimate=pl.CostEstimate(flops=flops, bytes_accessed=moved, transcendentals=0),
        )(*args)

    return run


def spec(block, index):
    return pl.BlockSpec(block, index)


def whole(x):
    return pl.BlockSpec(x.shape, lambda *_: (0,) * x.ndim)


SCALAR = pl.BlockSpec(memory_space=pltpu.SMEM)


def turned(x, row, n):
    part = x.shape[0] // n
    return jnp.concatenate([x[pl.ds(pl.multiple_of((row + j) % n * part, part), part)] for j in range(n)], axis=0)


def project(row, x, w, n_row):
    n, depth, width = w.shape
    part = x.shape[0] // n_row

    def kernel(row, x, w, *rest):
        outs, held = rest[:-1], rest[-1]

        @pl.when(pl.program_id(0) == 0)
        def _():
            held[...] = turned(x, row[0], n_row)

        total = dot(held[...], w[...])
        for j, out in enumerate(outs):
            out[...] = total[j * part : (j + 1) * part]

    return call(
        kernel,
        (n,),
        [SCALAR, whole(x), spec((None, depth, width), lambda a: (a, 0, 0))],
        [spec((part, width), lambda a: (0, a))] * n_row,
        [jax.ShapeDtypeStruct((part, n * width), F32)] * n_row,
        2 * x.shape[0] * n * depth * width,
        [pltpu.VMEM(x.shape, BF16)],
    )(row, x, w)


def back_context(row, mine, sib, w, n_row):
    width, depth = w.shape
    half = mine.shape[0]
    part = 2 * half // n_row

    def kernel(row, mine, sib, w, *rest):
        outs, total = rest[:-1], rest[-1]

        @pl.when(pl.program_id(0) == 0)
        def _():
            total[...] = jnp.zeros_like(total)

        total[:half] += dot(mine[...], w[...], NT)
        total[half:] += dot(sib[...], w[...], NT)

        @pl.when(pl.program_id(0) == pl.num_programs(0) - 1)
        def _():
            for j, out in enumerate(outs):
                out[...] = total[pl.ds(pl.multiple_of((row[0] + j) % n_row * part, part), part)]

    step = 2 * WIDE
    x_spec = spec((half, step), lambda k: (0, k))
    return call(
        kernel,
        (depth // step,),
        [SCALAR, x_spec, x_spec, spec((width, step), lambda k: (0, k))],
        [spec((part, width), lambda k: (0, 0))] * n_row,
        [jax.ShapeDtypeStruct((part, width), F32)] * n_row,
        4 * half * depth * width,
        [pltpu.VMEM((2 * half, width), F32)],
    )(row, mine, sib, w)


def place(row, *groups):
    n = len(groups[0])
    part, width = groups[0][0].shape

    def kernel(row, *refs):
        out = refs[-1]
        for i in range(len(groups)):
            for j in range(n):
                first = i * n * part + (row[0] + j) % n * part
                out[pl.ds(pl.multiple_of(first, part), part)] = refs[i * n + j][...]

    flat = [x for g in groups for x in g]
    shape = (len(groups) * n * part, width)
    return call(
        kernel,
        (1,),
        [SCALAR] + [whole(x) for x in flat],
        spec(shape, lambda _: (0, 0)),
        jax.ShapeDtypeStruct(shape, BF16),
        0,
    )(row, *flat)


def mix(context, context_sib, w, w_sib):
    width, depth = w.shape
    half = context_sib.shape[0]

    def kernel(c, cs, w, ws, out):
        out[...] = (dot(c[...], w[...]) + dot(cs[...], ws[...])).astype(BF16)

    step = 2 * WIDE
    c_spec = spec((half, width), lambda n: (0, 0))
    w_spec = spec((width, step), lambda n: (0, n))
    return call(
        kernel,
        (depth // step,),
        [c_spec, c_spec, w_spec, w_spec],
        spec((half, step), lambda n: (0, n)),
        jax.ShapeDtypeStruct((half, depth), BF16),
        4 * half * depth * width,
    )(context, context_sib, w, w_sib)


def back_tokens(grads, grads_sib, w, w_sib):
    n, depth, width = w.shape
    half = grads_sib.shape[1]

    def kernel(g, gs, w, ws, out):
        total = dot(g[0], w[0], NT) + dot(gs[0], ws[0], NT)
        for a in range(1, n):
            total = total + dot(g[a], w[a], NT) + dot(gs[a], ws[a], NT)
        out[...] = total.astype(BF16)

    g_spec = spec((n, half, width), lambda m: (0, 0, 0))
    w_spec = spec((n, WIDE, width), lambda m: (0, m, 0))
    return call(
        kernel,
        (depth // WIDE,),
        [g_spec, g_spec, w_spec, w_spec],
        spec((half, WIDE), lambda m: (0, m)),
        jax.ShapeDtypeStruct((half, depth), BF16),
        4 * half * n * depth * width,
    )(grads, grads_sib, w, w_sib)


def weight_qkv(row, mine, sib, other_mine, other_sib, grads, grads2):
    n, seq, width = grads.shape
    half, depth = mine.shape
    pieces, local = len(grads2), grads2[0].shape[1]

    def kernel(row, t0, t1, t2, t3, g, *rest):
        g2, out, held = rest[:pieces], rest[-2], rest[-1]

        @pl.when(pl.program_id(0) == 0)
        def _():
            held[:, :seq] = g[...]
            for j in range(pieces):
                first = seq + (row[0] + j) % pieces * local
                held[:, pl.ds(pl.multiple_of(first, local), local)] = g2[j][...]

        x = jnp.concatenate([t0[...], t1[...], t2[...], t3[...]], axis=0)
        for a in range(n):
            out[a] = dot(x, held[a], TN).astype(BF16)

    t_spec = spec((half, WIDE), lambda m: (0, m))
    return call(
        kernel,
        (depth // WIDE,),
        [SCALAR] + [t_spec] * 4 + [whole(grads)] + [whole(x) for x in grads2],
        spec((n, WIDE, width), lambda m: (0, m, 0)),
        jax.ShapeDtypeStruct((n, depth, width), BF16),
        4 * seq * n * depth * width,
        [pltpu.VMEM((n, 2 * seq, width), BF16)],
    )(row, mine, sib, other_mine, other_sib, grads, *grads2)


def weight_out(row, mine, sib, other_mine, other_sib, context, context2):
    seq, width = context.shape
    half, depth = mine.shape
    first_other = depth // WIDE
    pieces, local = len(context2), context2[0].shape[0]

    def kernel(row, t0, t1, t2, t3, c, *rest):
        c2, out, held = rest[:pieces], rest[-2], rest[-1]

        @pl.when(pl.program_id(0) == 0)
        def _():
            held[:, :seq] = c[...].T
            for j in range(pieces):
                first = seq + (row[0] + j) % pieces * local
                held[:, pl.ds(pl.multiple_of(first, local), local)] = c2[j][...].T

        x = jnp.concatenate([t0[...], t1[...], t2[...], t3[...]], axis=0)
        out[...] = dot(held[...], x).astype(BF16)

    t_spec = spec((half, WIDE), lambda m: (0, m))
    o_spec = spec((half, WIDE), lambda m: (0, first_other + m))
    return call(
        kernel,
        (depth // WIDE,),
        [SCALAR, t_spec, t_spec, o_spec, o_spec, whole(context)] + [whole(x) for x in context2],
        spec((width, WIDE), lambda m: (0, m)),
        jax.ShapeDtypeStruct((width, depth), BF16),
        4 * seq * depth * width,
        [pltpu.VMEM((width, 2 * seq), BF16)],
    )(row, mine, sib, other_mine, other_sib, context, *context2)


def soft_rows(q, k, rows, cols):
    scores = dot(q, k, NT) * (1.0 / DH**0.5)
    scores = jnp.where(rows >= cols, scores, -1e30)
    expo = jnp.exp(scores - jnp.max(scores, axis=-1, keepdims=True))
    return expo / jnp.sum(expo, axis=-1, keepdims=True)


def forward_kernel(rows, cols, q, k, v, context):
    probs = soft_rows(q[...], k[...], rows[...], cols[...])
    context[...] = dot(probs.astype(BF16), v[...]).astype(BF16)


def backward_kernel(rows, cols, q, k, v, g, out):
    scale = 1.0 / DH**0.5
    probs = soft_rows(q[...], k[...], rows[...], cols[...])
    out[2] = dot(probs.astype(BF16), g[...], TN).astype(BF16)
    grad_probs = dot(g[...], v[...], NT)
    delta = jnp.sum(grad_probs * probs, axis=-1, keepdims=True)
    grad_scores = (probs * (grad_probs - delta) * scale).astype(BF16)
    out[0] = dot(grad_scores, k[...]).astype(BF16)
    out[1] = dot(grad_scores, q[...], TN).astype(BF16)


def attention(rows, cols, qkv, grad_context=None):
    seq, width = qkv.shape[0], qkv.shape[1] // 3
    heads = width // DH

    def head(n, first):
        return spec((n, DH), lambda h: (0, first + h))

    ins = [whole(rows), whole(cols)] + [head(seq, a * heads) for a in range(3)]
    args = [rows, cols, qkv, qkv, qkv]
    if grad_context is None:
        return call(
            forward_kernel, (heads,), ins, head(seq, 0),
            jax.ShapeDtypeStruct((seq, width), BF16), 4 * heads * seq * seq * DH,
        )(*args)
    return call(
        backward_kernel, (heads,), ins + [head(seq, 0)], spec((3, seq, DH), lambda h: (0, 0, h)),
        jax.ShapeDtypeStruct((3, seq, width), BF16), 10 * heads * seq * seq * DH,
    )(*args, grad_context)


def after(x, *others):
    return lax.optimization_barrier((x, *others))[0]


def body(tokens, w_qkv, w_out, cotangent):
    n_row = lax.axis_size("row")
    n_col = lax.axis_size("colxdept")
    n_dp = lax.axis_size("dp")
    chips = n_col // 2
    tile = tokens.shape[1]
    seq = tile * n_col
    half, local = seq // 2, seq // n_row
    core = lax.axis_index("colxdept") % 2
    row = lax.axis_index("row").astype(jnp.int32)
    at = row[None]
    same_core = [list(range(c, n_col, 2)) for c in range(2)]

    def swap_cores(x):
        return lax.ppermute(x, "colxdept", [(i, i ^ 1) for i in range(n_col)])

    def swap_dp(x):
        return lax.ppermute(x, "dp", [(i, (i + 1) % n_dp) for i in range(n_dp)])

    def along_row(x, step):
        return lax.ppermute(x, "row", [(i, (i + step) % n_row) for i in range(n_row)])

    def among_chips(x):
        return lax.all_to_all(x, "colxdept", 0, 0, axis_index_groups=same_core)

    def gather_core(x):
        return among_chips(jnp.broadcast_to(x[None], (chips, *x.shape))).reshape(half, -1)

    def gather_row(x):
        return [x] + [along_row(x, -j) for j in range(1, n_row)]

    def sum_row(parts):
        total = parts[0]
        for j in range(1, n_row):
            total = total + along_row(parts[j], j)
        return total.astype(BF16)

    index = jnp.arange(seq, dtype=jnp.int32)
    owner = (index // half + core) % 2
    position = ((index % half) // tile * 2 + owner) * tile + index % tile
    rows, cols = position[:, None], position[None, :]

    tok_mine = gather_core(tokens[0])
    tok_sib = swap_cores(tok_mine)
    cot_mine = gather_core(after(cotangent[0], tok_mine))
    cot_sib = swap_cores(cot_mine)
    w_out_sib = swap_cores(w_out)
    w_qkv_sib = swap_cores(w_qkv)

    qkv_mine = gather_row(sum_row(project(at, tok_mine, w_qkv, n_row)))
    qkv_sib = gather_row(sum_row(project(at, tok_sib, w_qkv, n_row)))
    cot_sib_held = after(cot_sib, w_out_sib, w_qkv_sib)
    back_parts = back_context(at, cot_mine, cot_sib_held, w_out, n_row)
    grad_context = place(at, gather_row(sum_row(back_parts)))

    other = swap_dp(jnp.concatenate([after(tokens[0], cot_mine), cotangent[0]], axis=1))
    other_mine = gather_core(other)
    other_sib = swap_cores(other_mine)

    def from_other(x, axis):
        return gather_row(swap_dp(lax.dynamic_slice_in_dim(x, row * local, local, axis=axis)))

    def finish(part):
        parts = among_chips(part.reshape(chips, tile, -1))
        return jnp.sum(parts.astype(F32), axis=0).astype(BF16)

    qkv = place(at, qkv_mine, qkv_sib)
    context = attention(rows, cols, qkv)
    context_sib = swap_cores(context[half:])
    mixed = finish(mix(after(context, other_mine), context_sib, w_out, w_out_sib))
    context2 = from_other(context, 0)
    grad_out = weight_out(at, cot_mine, cot_sib, other_mine, other_sib, context, context2)

    grads = attention(rows, cols, qkv, grad_context)
    grads_sib = swap_cores(grads[:, half:])
    grads2 = from_other(grads, 1)
    grad_tokens = finish(back_tokens(grads, grads_sib, w_qkv, w_qkv_sib))
    grad_qkv = weight_qkv(at, tok_mine, tok_sib, other_mine, other_sib, grads, grads2)
    return (mixed[None], grad_tokens[None], grad_qkv, grad_out)


def solution(mesh):
    return jax.shard_map(
        body,
        mesh=mesh,
        in_specs=(
            P("dp", "colxdept", "row"),
            P(None, "row", "colxdept"),
            P("colxdept", "row"),
            P("dp", "colxdept", "row"),
        ),
        out_specs=(
            P("dp", "colxdept", "row"),
            P("dp", "colxdept", "row"),
            P(None, "row", "colxdept"),
            P("colxdept", "row"),
        ),
        check_vma=False,
    )
```

```python
import jax
import jax.numpy as jnp
from jax import lax
from jax.experimental import pallas as pl
from jax.experimental.pallas import tpu as pltpu
from jax.sharding import PartitionSpec as P

DH = 128
F32 = jnp.float32
BF16 = jnp.bfloat16
NT = (((1,), (1,)), ((), ()))
TN = (((0,), (0,)), ((), ()))
WIDE = 512


def dot(a, b, dims=None):
    if dims is None:
        return jnp.dot(a, b, preferred_element_type=F32)
    return lax.dot_general(a, b, dims, preferred_element_type=F32)


def call(kernel, grid, in_specs, out_specs, out_shape, flops, scratch=()):
    def run(*args):
        many = out_shape if isinstance(out_shape, list) else [out_shape]
        moved = sum(a.size * a.dtype.itemsize for a in [*args, *many])
        return pl.pallas_call(
            kernel,
            grid=grid,
            in_specs=in_specs,
            out_specs=out_specs,
            out_shape=out_shape,
            scratch_shapes=list(scratch),
            compiler_params=pltpu.CompilerParams(vmem_limit_bytes=48 * 2**20),
            cost_estimate=pl.CostEstimate(flops=flops, bytes_accessed=moved, transcendentals=0),
        )(*args)

    return run


def spec(block, index):
    return pl.BlockSpec(block, index)


def whole(x):
    return pl.BlockSpec(x.shape, lambda *_: (0,) * x.ndim)


SCALAR = pl.BlockSpec(memory_space=pltpu.SMEM)


def turned(x, row, n):
    part = x.shape[0] // n
    return jnp.concatenate([x[pl.ds(pl.multiple_of((row + j) % n * part, part), part)] for j in range(n)], axis=0)


def project(row, x, w, n_row):
    n, depth, width = w.shape
    part = x.shape[0] // n_row

    def kernel(row, x, w, *rest):
        outs, held = rest[:-1], rest[-1]

        @pl.when(pl.program_id(0) == 0)
        def _():
            held[...] = turned(x, row[0], n_row)

        total = dot(held[...], w[...])
        for j, out in enumerate(outs):
            out[...] = total[j * part : (j + 1) * part]

    return call(
        kernel,
        (n,),
        [SCALAR, whole(x), spec((None, depth, width), lambda a: (a, 0, 0))],
        [spec((part, width), lambda a: (0, a))] * n_row,
        [jax.ShapeDtypeStruct((part, n * width), F32)] * n_row,
        2 * x.shape[0] * n * depth * width,
        [pltpu.VMEM(x.shape, BF16)],
    )(row, x, w)


def back_context(row, mine, sib, w, n_row):
    width, depth = w.shape
    half = mine.shape[0]
    part = 2 * half // n_row

    def kernel(row, mine, sib, w, *rest):
        outs, total = rest[:-1], rest[-1]

        @pl.when(pl.program_id(0) == 0)
        def _():
            total[...] = jnp.zeros_like(total)

        total[:half] += dot(mine[...], w[...], NT)
        total[half:] += dot(sib[...], w[...], NT)

        @pl.when(pl.program_id(0) == pl.num_programs(0) - 1)
        def _():
            for j, out in enumerate(outs):
                out[...] = total[pl.ds(pl.multiple_of((row[0] + j) % n_row * part, part), part)]

    step = 2 * WIDE
    x_spec = spec((half, step), lambda k: (0, k))
    return call(
        kernel,
        (depth // step,),
        [SCALAR, x_spec, x_spec, spec((width, step), lambda k: (0, k))],
        [spec((part, width), lambda k: (0, 0))] * n_row,
        [jax.ShapeDtypeStruct((part, width), F32)] * n_row,
        4 * half * depth * width,
        [pltpu.VMEM((2 * half, width), F32)],
    )(row, mine, sib, w)


def place(row, pieces, halves):
    n = len(pieces)
    rows, width = pieces[0].shape
    part = rows // halves

    def kernel(row, *refs):
        out = refs[-1]
        for j in range(n):
            for i in range(halves):
                first = i * n * part + (row[0] + j) % n * part
                out[pl.ds(pl.multiple_of(first, part), part)] = refs[j][i * part : (i + 1) * part]

    shape = (n * rows, width)
    return call(
        kernel,
        (1,),
        [SCALAR] + [whole(x) for x in pieces],
        spec(shape, lambda _: (0, 0)),
        jax.ShapeDtypeStruct(shape, BF16),
        0,
    )(row, *pieces)


def mix(context, context_sib, w, w_sib):
    width, depth = w.shape
    half = context_sib.shape[0]

    def kernel(c, cs, w, ws, out):
        out[...] = (dot(c[...], w[...]) + dot(cs[...], ws[...])).astype(BF16)

    step = 2 * WIDE
    c_spec = spec((half, width), lambda n: (0, 0))
    w_spec = spec((width, step), lambda n: (0, n))
    return call(
        kernel,
        (depth // step,),
        [c_spec, c_spec, w_spec, w_spec],
        spec((half, step), lambda n: (0, n)),
        jax.ShapeDtypeStruct((half, depth), BF16),
        4 * half * depth * width,
    )(context, context_sib, w, w_sib)


def back_tokens(grads, grads_sib, w, w_sib):
    n, depth, width = w.shape
    half = grads_sib.shape[1]

    def kernel(g, gs, w, ws, out):
        total = dot(g[0], w[0], NT) + dot(gs[0], ws[0], NT)
        for a in range(1, n):
            total = total + dot(g[a], w[a], NT) + dot(gs[a], ws[a], NT)
        out[...] = total.astype(BF16)

    g_spec = spec((n, half, width), lambda m: (0, 0, 0))
    w_spec = spec((n, WIDE, width), lambda m: (0, m, 0))
    return call(
        kernel,
        (depth // WIDE,),
        [g_spec, g_spec, w_spec, w_spec],
        spec((half, WIDE), lambda m: (0, m)),
        jax.ShapeDtypeStruct((half, depth), BF16),
        4 * half * n * depth * width,
    )(grads, grads_sib, w, w_sib)


def weight_qkv(row, mine, sib, other_mine, other_sib, grads, grads2):
    n, seq, width = grads.shape
    half, depth = mine.shape
    pieces, local = len(grads2), grads2[0].shape[1]

    def kernel(row, t0, t1, t2, t3, g, *rest):
        g2, out, held = rest[:pieces], rest[-2], rest[-1]

        @pl.when(pl.program_id(0) == 0)
        def _():
            held[:, :seq] = g[...]
            for j in range(pieces):
                first = seq + (row[0] + j) % pieces * local
                held[:, pl.ds(pl.multiple_of(first, local), local)] = g2[j][...]

        x = jnp.concatenate([t0[...], t1[...], t2[...], t3[...]], axis=0)
        for a in range(n):
            out[a] = dot(x, held[a], TN).astype(BF16)

    t_spec = spec((half, WIDE), lambda m: (0, m))
    return call(
        kernel,
        (depth // WIDE,),
        [SCALAR] + [t_spec] * 4 + [whole(grads)] + [whole(x) for x in grads2],
        spec((n, WIDE, width), lambda m: (0, m, 0)),
        jax.ShapeDtypeStruct((n, depth, width), BF16),
        4 * seq * n * depth * width,
        [pltpu.VMEM((n, 2 * seq, width), BF16)],
    )(row, mine, sib, other_mine, other_sib, grads, *grads2)


def weight_out(row, mine, sib, other_mine, other_sib, context, context2):
    seq, width = context.shape
    half, depth = mine.shape
    first_other = depth // WIDE
    pieces, local = len(context2), context2[0].shape[0]

    def kernel(row, t0, t1, t2, t3, c, *rest):
        c2, out, held = rest[:pieces], rest[-2], rest[-1]

        @pl.when(pl.program_id(0) == 0)
        def _():
            held[:, :seq] = c[...].T
            for j in range(pieces):
                first = seq + (row[0] + j) % pieces * local
                held[:, pl.ds(pl.multiple_of(first, local), local)] = c2[j][...].T

        x = jnp.concatenate([t0[...], t1[...], t2[...], t3[...]], axis=0)
        out[...] = dot(held[...], x).astype(BF16)

    t_spec = spec((half, WIDE), lambda m: (0, m))
    o_spec = spec((half, WIDE), lambda m: (0, first_other + m))
    return call(
        kernel,
        (depth // WIDE,),
        [SCALAR, t_spec, t_spec, o_spec, o_spec, whole(context)] + [whole(x) for x in context2],
        spec((width, WIDE), lambda m: (0, m)),
        jax.ShapeDtypeStruct((width, depth), BF16),
        4 * seq * depth * width,
        [pltpu.VMEM((width, 2 * seq), BF16)],
    )(row, mine, sib, other_mine, other_sib, context, *context2)


def soft_rows(q, k, rows, cols):
    scores = dot(q, k, NT) * (1.0 / DH**0.5)
    scores = jnp.where(rows >= cols, scores, -1e30)
    expo = jnp.exp(scores - jnp.max(scores, axis=-1, keepdims=True))
    return expo / jnp.sum(expo, axis=-1, keepdims=True)


def forward_kernel(rows, cols, q, k, v, context):
    probs = soft_rows(q[...], k[...], rows[...], cols[...])
    context[...] = dot(probs.astype(BF16), v[...]).astype(BF16)


def backward_kernel(rows, cols, q, k, v, g, out):
    scale = 1.0 / DH**0.5
    probs = soft_rows(q[...], k[...], rows[...], cols[...])
    out[2] = dot(probs.astype(BF16), g[...], TN).astype(BF16)
    grad_probs = dot(g[...], v[...], NT)
    delta = jnp.sum(grad_probs * probs, axis=-1, keepdims=True)
    grad_scores = (probs * (grad_probs - delta) * scale).astype(BF16)
    out[0] = dot(grad_scores, k[...]).astype(BF16)
    out[1] = dot(grad_scores, q[...], TN).astype(BF16)


def attention(rows, cols, qkv, grad_context=None):
    seq, width = qkv.shape[0], qkv.shape[1] // 3
    heads = width // DH

    def head(n, first):
        return spec((n, DH), lambda h: (0, first + h))

    ins = [whole(rows), whole(cols)] + [head(seq, a * heads) for a in range(3)]
    args = [rows, cols, qkv, qkv, qkv]
    if grad_context is None:
        return call(
            forward_kernel, (heads,), ins, head(seq, 0),
            jax.ShapeDtypeStruct((seq, width), BF16), 4 * heads * seq * seq * DH,
        )(*args)
    return call(
        backward_kernel, (heads,), ins + [head(seq, 0)], spec((3, seq, DH), lambda h: (0, 0, h)),
        jax.ShapeDtypeStruct((3, seq, width), BF16), 10 * heads * seq * seq * DH,
    )(*args, grad_context)


def after(x, *others):
    return lax.optimization_barrier((x, *others))[0]


def body(tokens, w_qkv, w_out, cotangent):
    n_row = lax.axis_size("row")
    n_col = lax.axis_size("colxdept")
    n_dp = lax.axis_size("dp")
    chips = n_col // 2
    tile = tokens.shape[1]
    seq = tile * n_col
    half, local = seq // 2, seq // n_row
    core = lax.axis_index("colxdept") % 2
    row = lax.axis_index("row").astype(jnp.int32)
    at = row[None]
    same_core = [list(range(c, n_col, 2)) for c in range(2)]

    def swap_cores(x):
        return lax.ppermute(x, "colxdept", [(i, i ^ 1) for i in range(n_col)])

    def swap_dp(x):
        return lax.ppermute(x, "dp", [(i, (i + 1) % n_dp) for i in range(n_dp)])

    def along_row(x, step):
        return lax.ppermute(x, "row", [(i, (i + step) % n_row) for i in range(n_row)])

    def among_chips(x):
        return lax.all_to_all(x, "colxdept", 0, 0, axis_index_groups=same_core)

    def gather_core(x):
        return among_chips(jnp.broadcast_to(x[None], (chips, *x.shape))).reshape(half, -1)

    def gather_row(x):
        return [x] + [along_row(x, -j) for j in range(1, n_row)]

    def sum_row(parts):
        total = parts[0]
        for j in range(1, n_row):
            total = total + along_row(parts[j], j)
        return total.astype(BF16)

    index = jnp.arange(seq, dtype=jnp.int32)
    owner = (index // half + core) % 2
    position = ((index % half) // tile * 2 + owner) * tile + index % tile
    rows, cols = position[:, None], position[None, :]

    w_out_sib = swap_cores(w_out)
    w_qkv_sib = swap_cores(w_qkv)
    tok_mine, w_out_sib, w_qkv_sib = lax.optimization_barrier((gather_core(tokens[0]), w_out_sib, w_qkv_sib))
    tok_sib = swap_cores(tok_mine)
    cot_mine = gather_core(after(cotangent[0], tok_mine))
    other = swap_dp(jnp.concatenate([after(tokens[0], tok_mine), cotangent[0]], axis=1))

    mine_parts = project(at, tok_mine, w_qkv, n_row)
    sib_parts = project(at, after(tok_sib, *mine_parts), w_qkv, n_row)
    mine_sum = sum_row([after(mine_parts[0], *sib_parts), *mine_parts[1:]])
    cot_mine = after(cot_mine, mine_sum)
    cot_sib = swap_cores(cot_mine)
    back_parts = back_context(at, cot_mine, cot_sib, w_out, n_row)
    both = jnp.concatenate([mine_sum, sum_row(sib_parts)], axis=0)
    pieces = gather_row(after(both, *back_parts))
    back_sum = sum_row(back_parts)
    back_pieces = gather_row(back_sum)

    other_mine = gather_core(after(other, cot_mine))

    def to_other(x, axis):
        return swap_dp(lax.dynamic_slice_in_dim(x, row * local, local, axis=axis))

    def finish(part, *others):
        parts = after(among_chips(part.reshape(chips, tile, -1)), *others)
        return jnp.sum(parts.astype(F32), axis=0).astype(BF16)

    qkv = after(place(at, pieces, 2), back_sum)
    context = attention(rows, cols, qkv)
    context_sib = swap_cores(context[half:])
    context2 = to_other(context, 0)
    other_sib = swap_cores(after(other_mine, context))
    mix_part = mix(after(context, *back_pieces), context_sib, w_out, w_out_sib)
    grad_context = after(place(at, back_pieces, 1), mix_part)
    grads = attention(rows, cols, qkv, grad_context)
    grads_sib = swap_cores(grads[:, half:])
    grads2 = to_other(grads, 1)
    grad_out = weight_out(at, cot_mine, cot_sib, other_mine, other_sib, context, gather_row(context2))
    grads_sib, grads2, _ = lax.optimization_barrier((grads_sib, grads2, grad_out))
    tokens_part = back_tokens(grads, grads_sib, w_qkv, w_qkv_sib)
    mixed = finish(after(mix_part, other_mine, context2), tokens_part)
    tokens_part = after(tokens_part, mixed)
    grad_qkv = weight_qkv(at, tok_mine, tok_sib, other_mine, other_sib, grads, gather_row(grads2))
    grad_tokens = finish(tokens_part, grad_qkv)
    return (mixed[None], grad_tokens[None], grad_qkv, grad_out)


def solution(mesh):
    return jax.shard_map(
        body,
        mesh=mesh,
        in_specs=(
            P("dp", "colxdept", "row"),
            P(None, "row", "colxdept"),
            P("colxdept", "row"),
            P("dp", "colxdept", "row"),
        ),
        out_specs=(
            P("dp", "colxdept", "row"),
            P("dp", "colxdept", "row"),
            P(None, "row", "colxdept"),
            P("colxdept", "row"),
        ),
        check_vma=False,
    )
```

```python
import jax
import jax.numpy as jnp
from jax import lax
from jax.experimental import pallas as pl
from jax.experimental.pallas import tpu as pltpu
from jax.sharding import PartitionSpec as P

DH = 128
F32 = jnp.float32
BF16 = jnp.bfloat16
NT = (((1,), (1,)), ((), ()))
TN = (((0,), (0,)), ((), ()))
MIB = 2**20


def dot(a, b, dims=None):
    if dims is None:
        return jnp.dot(a, b, preferred_element_type=F32)
    return lax.dot_general(a, b, dims, preferred_element_type=F32)


def call(kernel, grid, in_specs, out_specs, out_shape, flops, scratch=(), room=24):
    def run(*args):
        many = out_shape if isinstance(out_shape, list) else [out_shape]
        moved = sum(a.size * a.dtype.itemsize for a in [*args, *many])
        return pl.pallas_call(
            kernel,
            grid=grid,
            in_specs=in_specs,
            out_specs=out_specs,
            out_shape=out_shape,
            scratch_shapes=list(scratch),
            compiler_params=pltpu.CompilerParams(vmem_limit_bytes=room * MIB),
            cost_estimate=pl.CostEstimate(flops=flops, bytes_accessed=moved, transcendentals=0),
        )(*args)

    return run


def spec(block, index):
    return pl.BlockSpec(block, index)


def whole(x):
    return pl.BlockSpec(x.shape, lambda *_: (0,) * x.ndim)


SCALAR = pl.BlockSpec(memory_space=pltpu.SMEM)


def nth_part(row, j, n, part):
    return pl.ds(pl.multiple_of((row[0] + j) % n * part, part), part)


def project(mine, sib, w):
    n, depth, width = w.shape
    half = mine.shape[0]

    x_spec = spec((half, depth), lambda a: (0, 0))

    def kernel(mine, sib, w, out):
        out[:half] = dot(mine[...], w[...])
        out[half:] = dot(sib[...], w[...])

    return call(
        kernel,
        (n,),
        [x_spec, x_spec, spec((None, depth, width), lambda a: (a, 0, 0))],
        spec((2 * half, width), lambda a: (0, a)),
        jax.ShapeDtypeStruct((2 * half, n * width), F32),
        4 * half * n * depth * width,
    )(mine, sib, w)


def back_context(mine, sib, w):
    width, depth = w.shape
    half = mine.shape[0]

    def kernel(mine, sib, w, out):
        @pl.when(pl.program_id(0) == 0)
        def _():
            out[...] = jnp.zeros_like(out)

        out[:half] += dot(mine[...], w[...], NT)
        out[half:] += dot(sib[...], w[...], NT)

    step = min(1024, depth)
    steps = depth // step
    x_spec = spec((half, step), lambda k: (0, steps + k))
    return call(
        kernel,
        (depth // step,),
        [x_spec, x_spec, spec((width, step), lambda k: (0, k))],
        spec((2 * half, width), lambda k: (0, 0)),
        jax.ShapeDtypeStruct((2 * half, width), F32),
        4 * half * depth * width,
    )(mine, sib, w)


def place(row, left, right):
    n = len(left)
    part, split = left[0].shape
    shape = (n * part, split + right[0].shape[1])

    def kernel(row, *refs):
        out = refs[-1]
        for j in range(n):
            rows = nth_part(row, j, n, part)
            out[rows, :split] = refs[j][...]
            out[rows, split:] = refs[n + j][...]

    flat = [*left, *right]
    return call(
        kernel,
        (1,),
        [SCALAR] + [whole(x) for x in flat],
        spec(shape, lambda _: (0, 0)),
        jax.ShapeDtypeStruct(shape, BF16),
        0,
    )(row, *flat)


def attention(rows, cols, held):
    seq, width = held.shape[0], held.shape[1] // 4
    heads = width // DH
    scale = 1.0 / DH**0.5

    def kernel(rows, cols, q, k, v, g, out):
        scores = dot(q[...], k[...], NT) * scale
        scores = jnp.where(rows[...] >= cols[...], scores, -1e30)
        expo = jnp.exp(scores - jnp.max(scores, axis=-1, keepdims=True))
        probs = expo / jnp.sum(expo, axis=-1, keepdims=True)
        probs_b = probs.astype(BF16)
        out[0] = dot(probs_b, v[...]).astype(BF16)
        out[3] = dot(probs_b, g[...], TN).astype(BF16)
        grad_probs = dot(g[...], v[...], NT)
        delta = jnp.sum(grad_probs * probs, axis=-1, keepdims=True)
        grad_scores = (probs * (grad_probs - delta) * scale).astype(BF16)
        out[1] = dot(grad_scores, k[...]).astype(BF16)
        out[2] = dot(grad_scores, q[...], TN).astype(BF16)

    def head(a):
        return spec((seq, DH), lambda h: (0, a * heads + h))

    return call(
        kernel,
        (heads,),
        [whole(rows), whole(cols)] + [head(a) for a in range(4)],
        spec((4, seq, DH), lambda h: (0, 0, h)),
        jax.ShapeDtypeStruct((4, seq, width), BF16),
        14 * heads * seq * seq * DH,
    )(rows, cols, held, held, held, held)


def partials(chips, done, done_sib, w_out, w_out_sib, w_qkv, w_qkv_sib):
    n, depth, width = w_qkv.shape
    half = done_sib.shape[1]
    step = min(512, depth)

    def side(x, first):
        return jnp.concatenate([x[a] for a in range(first, n + first)], axis=1)

    def kernel(d, ds, wo, wos, wq, wqs, out):
        mixed = dot(d[0], wo[...]) + dot(ds[0], wos[...])
        out[:, 0] = mixed.astype(BF16).reshape(out.shape[0], *out.shape[2:])
        grads = jnp.concatenate([side(d, 1), side(ds, 1)], axis=1)
        weights = jnp.concatenate([side(wq, 0), side(wqs, 0)], axis=1)
        out[:, 1] = dot(grads, weights, NT).astype(BF16).reshape(out.shape[0], *out.shape[2:])

    d_spec = spec((n + 1, half, width), lambda m: (0, 0, 0))
    o_spec = spec((width, step), lambda m: (0, m))
    q_spec = spec((n, step, width), lambda m: (0, m, 0))
    return call(
        kernel,
        (depth // step,),
        [d_spec, d_spec, o_spec, o_spec, q_spec, q_spec],
        spec((chips, 2, half // chips, step), lambda m: (0, 0, 0, m)),
        jax.ShapeDtypeStruct((chips, 2, half // chips, depth), BF16),
        4 * half * (n + 1) * depth * width,
        room=32,
    )(done, done_sib, w_out, w_out_sib, w_qkv, w_qkv_sib)


def weight_qkv(row, mine, sib, other_mine, other_sib, done, done2):
    n, seq, width = done.shape[0] - 1, *done.shape[1:]
    half, depth = mine.shape[0], mine.shape[1] // 2
    pieces, part = len(done2), done2[0].shape[1]
    step = min(1024, depth)

    def kernel(row, t0, t1, t2, t3, d, *rest):
        d2, out, held = rest[:pieces], rest[-2], rest[-1]

        @pl.when(pl.program_id(0) == 0)
        def _():
            for a in range(n):
                columns = slice(a * width, (a + 1) * width)
                held[0, :, columns] = d[a + 1]
                for j in range(pieces):
                    held[1, nth_part(row, j, pieces, part), columns] = d2[j][a + 1]

        x = jnp.concatenate([t0[...], t1[...], t2[...], t3[...]], axis=0)
        total = dot(x, held[...].reshape(2 * seq, n * width), TN)
        for a in range(n):
            out[a] = total[:, a * width : (a + 1) * width].astype(BF16)

    t_spec = spec((half, step), lambda m: (0, m))
    return call(
        kernel,
        (depth // step,),
        [SCALAR] + [t_spec] * 4 + [whole(done)] + [whole(x) for x in done2],
        spec((n, step, width), lambda m: (0, m, 0)),
        jax.ShapeDtypeStruct((n, depth, width), BF16),
        4 * seq * n * depth * width,
        [pltpu.VMEM((2, seq, n * width), BF16)],
        room=40,
    )(row, mine, sib, other_mine, other_sib, done, *done2)


def weight_out(row, mine, sib, other_mine, other_sib, done, done2):
    seq, width = done.shape[1:]
    half, depth = mine.shape[0], mine.shape[1] // 2
    pieces, part = len(done2), done2[0].shape[1]
    step = min(1024, depth)
    first = depth // step

    def kernel(row, t0, t1, t2, t3, c, *rest):
        c2, out, held = rest[:pieces], rest[-2], rest[-1]

        @pl.when(pl.program_id(0) == 0)
        def _():
            held[0] = c[...].T
            for j in range(pieces):
                held[1, :, nth_part(row, j, pieces, part)] = c2[j][...].T

        total = dot(held[0], jnp.concatenate([t0[...], t1[...]], axis=0))
        total = total + dot(held[1], jnp.concatenate([t2[...], t3[...]], axis=0))
        out[...] = total.astype(BF16)

    t_spec = spec((half, step), lambda m: (0, first + m))
    return call(
        kernel,
        (depth // step,),
        [SCALAR] + [t_spec] * 4 + [spec((None, seq, width), lambda m: (0, 0, 0))]
        + [spec((None, part, width), lambda m: (0, 0, 0))] * pieces,
        spec((width, step), lambda m: (0, m)),
        jax.ShapeDtypeStruct((width, depth), BF16),
        4 * seq * depth * width,
        [pltpu.VMEM((2, width, seq), BF16)],
        room=32,
    )(row, mine, sib, other_mine, other_sib, done, *done2)


def after(x, *others):
    return lax.optimization_barrier((x, *others))[0]


def body(tokens, w_qkv, w_out, cotangent):
    n_row = lax.axis_size("row")
    n_col = lax.axis_size("colxdept")
    n_dp = lax.axis_size("dp")
    chips = n_col // 2
    tile = tokens.shape[1]
    seq = tile * n_col
    half, local = seq // 2, seq // n_row
    core = lax.axis_index("colxdept") % 2
    row = lax.axis_index("row").astype(jnp.int32)
    at = row[None]
    same_core = [list(range(c, n_col, 2)) for c in range(2)]

    def swap_cores(x):
        return lax.ppermute(x, "colxdept", [(i, i ^ 1) for i in range(n_col)])

    def swap_dp(x):
        return lax.ppermute(x, "dp", [(i, (i + 1) % n_dp) for i in range(n_dp)])

    def along_row(x, step):
        return lax.ppermute(x, "row", [(i, (i + step) % n_row) for i in range(n_row)])

    def among_chips(x):
        return lax.all_to_all(x, "colxdept", 0, 0, axis_index_groups=same_core)

    def gather_core(x):
        return among_chips(jnp.broadcast_to(x[None], (chips, *x.shape))).reshape(half, -1)

    def gather_row(x):
        return [x] + [along_row(x, -j) for j in range(1, n_row)]

    def sum_row(x):
        return lax.psum_scatter(x, "row", scatter_dimension=0, tiled=True).astype(BF16)

    index = jnp.arange(seq, dtype=jnp.int32)
    owner = (index // half + core) % 2
    position = ((index % half) // tile * 2 + owner) * tile + index % tile
    rows, cols = position[:, None], position[None, :]

    w_out_sib = swap_cores(w_out)
    w_qkv_sib = swap_cores(w_qkv)
    own = jnp.concatenate([tokens[0], cotangent[0]], axis=1)
    mine, w_out_sib, w_qkv_sib = lax.optimization_barrier((gather_core(own), w_out_sib, w_qkv_sib))
    sib = swap_cores(mine)
    qkv_part = project(mine, sib, w_qkv)
    back_part = back_context(mine, sib, w_out)

    other = swap_dp(after(own, mine))
    other_mine = gather_core(after(other, back_part))

    pieces = gather_row(sum_row(qkv_part))
    back_pieces = gather_row(sum_row(back_part))
    done = attention(rows, cols, place(at, pieces, back_pieces))
    done_sib = swap_cores(done[:, half:])
    quarter = swap_dp(lax.dynamic_slice_in_dim(done, row * local, local, axis=1))
    done_sib, quarter, other_mine = lax.optimization_barrier((done_sib, quarter, other_mine))
    other_sib = swap_cores(other_mine)
    part = partials(chips, done, done_sib, w_out, w_out_sib, w_qkv, w_qkv_sib)
    shares = among_chips(part)
    done2 = gather_row(quarter)
    grad_out = weight_out(at, mine, sib, other_mine, other_sib, done, done2)
    grad_qkv = weight_qkv(at, mine, sib, other_mine, other_sib, done, done2)
    shares = after(shares, grad_out, grad_qkv)
    results = jnp.sum(shares.astype(F32), axis=0).astype(BF16)
    return (results[:1], results[1:], grad_qkv, grad_out)


def solution(mesh):
    return jax.shard_map(
        body,
        mesh=mesh,
        in_specs=(
            P("dp", "colxdept", "row"),
            P(None, "row", "colxdept"),
            P("colxdept", "row"),
            P("dp", "colxdept", "row"),
        ),
        out_specs=(
            P("dp", "colxdept", "row"),
            P("dp", "colxdept", "row"),
            P(None, "row", "colxdept"),
            P("colxdept", "row"),
        ),
        check_vma=False,
    )
```

```python
import jax
import jax.numpy as jnp
from jax import lax
from jax.experimental import pallas as pl
from jax.experimental.pallas import tpu as pltpu
from jax.sharding import PartitionSpec as P

DH = 128
F32 = jnp.float32
BF16 = jnp.bfloat16
NT = (((1,), (1,)), ((), ()))
TN = (((0,), (0,)), ((), ()))
ROOM = 56 * 2**20


def dot(a, b, dims=None):
    if dims is None:
        return jnp.dot(a, b, preferred_element_type=F32)
    return lax.dot_general(a, b, dims, preferred_element_type=F32)


def call(kernel, grid, in_specs, out_specs, out_shape, flops, scratch=()):
    def run(*args):
        many = out_shape if isinstance(out_shape, list) else [out_shape]
        moved = sum(a.size * a.dtype.itemsize for a in [*args, *many])
        return pl.pallas_call(
            kernel,
            grid=grid,
            in_specs=in_specs,
            out_specs=out_specs,
            out_shape=out_shape,
            scratch_shapes=list(scratch),
            compiler_params=pltpu.CompilerParams(vmem_limit_bytes=ROOM),
            cost_estimate=pl.CostEstimate(flops=flops, bytes_accessed=moved, transcendentals=0),
        )(*args)

    return run


def spec(block, index):
    return pl.BlockSpec(block, index)


def whole(x):
    return pl.BlockSpec(x.shape, lambda *_: (0,) * x.ndim)


SCALAR = pl.BlockSpec(memory_space=pltpu.SMEM)


def nth_part(row, j, n, part):
    return pl.ds(pl.multiple_of((row[0] + j) % n * part, part), part)


def project(mine, sib, w):
    n, depth, width = w.shape
    half = mine.shape[0]

    def kernel(mine, sib, w, out):
        out[:half] = dot(mine[...], w[...])
        out[half:] = dot(sib[...], w[...])

    return call(
        kernel,
        (n,),
        [whole(mine), whole(sib), spec((None, depth, width), lambda a: (a, 0, 0))],
        spec((2 * half, width), lambda a: (0, a)),
        jax.ShapeDtypeStruct((2 * half, n * width), F32),
        4 * half * n * depth * width,
    )(mine, sib, w)


def back_context(row, mine, sib, w, n_row):
    width, depth = w.shape
    half = mine.shape[0]
    part = 2 * half // n_row

    def kernel(row, mine, sib, w, *rest):
        outs, total = rest[:-1], rest[-1]

        @pl.when(pl.program_id(0) == 0)
        def _():
            total[...] = jnp.zeros_like(total)

        total[:half] += dot(mine[...], w[...], NT)
        total[half:] += dot(sib[...], w[...], NT)

        @pl.when(pl.program_id(0) == pl.num_programs(0) - 1)
        def _():
            for j, out in enumerate(outs):
                out[...] = total[nth_part(row, j, n_row, part)]

    step = min(1024, depth)
    x_spec = spec((half, step), lambda k: (0, k))
    return call(
        kernel,
        (depth // step,),
        [SCALAR, x_spec, x_spec, spec((width, step), lambda k: (0, k))],
        [spec((part, width), lambda k: (0, 0))] * n_row,
        [jax.ShapeDtypeStruct((part, width), F32)] * n_row,
        4 * half * depth * width,
        [pltpu.VMEM((2 * half, width), F32)],
    )(row, mine, sib, w)


def place(row, left, right):
    n = len(left)
    part, split = left[0].shape
    shape = (n * part, split + right[0].shape[1])

    def kernel(row, *refs):
        out = refs[-1]
        for j in range(n):
            rows = nth_part(row, j, n, part)
            out[rows, :split] = refs[j][...]
            out[rows, split:] = refs[n + j][...]

    flat = [*left, *right]
    return call(
        kernel,
        (1,),
        [SCALAR] + [whole(x) for x in flat],
        spec(shape, lambda _: (0, 0)),
        jax.ShapeDtypeStruct(shape, BF16),
        0,
    )(row, *flat)


def attention(rows, cols, held):
    seq, width = held.shape[0], held.shape[1] // 4
    heads = width // DH
    scale = 1.0 / DH**0.5

    def kernel(rows, cols, q, k, v, g, out):
        scores = dot(q[...], k[...], NT) * scale
        scores = jnp.where(rows[...] >= cols[...], scores, -1e30)
        expo = jnp.exp(scores - jnp.max(scores, axis=-1, keepdims=True))
        probs = expo / jnp.sum(expo, axis=-1, keepdims=True)
        probs_b = probs.astype(BF16)
        out[0] = dot(probs_b, v[...]).astype(BF16)
        out[3] = dot(probs_b, g[...], TN).astype(BF16)
        grad_probs = dot(g[...], v[...], NT)
        delta = jnp.sum(grad_probs * probs, axis=-1, keepdims=True)
        grad_scores = (probs * (grad_probs - delta) * scale).astype(BF16)
        out[1] = dot(grad_scores, k[...]).astype(BF16)
        out[2] = dot(grad_scores, q[...], TN).astype(BF16)

    def head(a):
        return spec((seq, DH), lambda h: (0, a * heads + h))

    return call(
        kernel,
        (heads,),
        [whole(rows), whole(cols)] + [head(a) for a in range(4)],
        spec((4, seq, DH), lambda h: (0, 0, h)),
        jax.ShapeDtypeStruct((4, seq, width), BF16),
        14 * heads * seq * seq * DH,
    )(rows, cols, held, held, held, held)


def partials(chips, done, done_sib, w_out, w_out_sib, w_qkv, w_qkv_sib):
    n, depth, width = w_qkv.shape
    half = done_sib.shape[1]
    step = min(512, depth)

    def side(x, first):
        return jnp.concatenate([x[a] for a in range(first, n + first)], axis=1)

    def kernel(d, ds, wo, wos, wq, wqs, out):
        mixed = dot(d[0], wo[...]) + dot(ds[0], wos[...])
        out[:, 0] = mixed.astype(BF16).reshape(out.shape[0], *out.shape[2:])
        grads = jnp.concatenate([side(d, 1), side(ds, 1)], axis=1)
        weights = jnp.concatenate([side(wq, 0), side(wqs, 0)], axis=1)
        out[:, 1] = dot(grads, weights, NT).astype(BF16).reshape(out.shape[0], *out.shape[2:])

    d_spec = spec((n + 1, half, width), lambda m: (0, 0, 0))
    o_spec = spec((width, step), lambda m: (0, m))
    q_spec = spec((n, step, width), lambda m: (0, m, 0))
    return call(
        kernel,
        (depth // step,),
        [d_spec, d_spec, o_spec, o_spec, q_spec, q_spec],
        spec((chips, 2, half // chips, step), lambda m: (0, 0, 0, m)),
        jax.ShapeDtypeStruct((chips, 2, half // chips, depth), BF16),
        4 * half * (n + 1) * depth * width,
    )(done, done_sib, w_out, w_out_sib, w_qkv, w_qkv_sib)


def weight_qkv(mine, sib, other_mine, other_sib, done, done2):
    n, seq, width = done.shape[0] - 1, *done.shape[1:]
    half, depth = mine.shape
    pieces, part = done2.shape[0], done2.shape[2]
    step = min(1024, depth)

    def kernel(t0, t1, t2, t3, d, d2, out, held):
        @pl.when(pl.program_id(0) == 0)
        def _():
            for a in range(n):
                columns = slice(a * width, (a + 1) * width)
                held[0, :, columns] = d[a + 1]
                for j in range(pieces):
                    held[1, j * part : (j + 1) * part, columns] = d2[j, a + 1]

        x = jnp.concatenate([t0[...], t1[...], t2[...], t3[...]], axis=0)
        total = dot(x, held[...].reshape(2 * seq, n * width), TN)
        for a in range(n):
            out[a] = total[:, a * width : (a + 1) * width].astype(BF16)

    t_spec = spec((half, step), lambda m: (0, m))
    return call(
        kernel,
        (depth // step,),
        [t_spec] * 4 + [whole(done), whole(done2)],
        spec((n, step, width), lambda m: (0, m, 0)),
        jax.ShapeDtypeStruct((n, depth, width), BF16),
        4 * seq * n * depth * width,
        [pltpu.VMEM((2, seq, n * width), BF16)],
    )(mine, sib, other_mine, other_sib, done, done2)


def weight_out(mine, sib, other_mine, other_sib, done, done2):
    seq, width = done.shape[1:]
    half, depth = mine.shape
    pieces, part = done2.shape[0], done2.shape[2]
    step = min(1024, depth)
    first = depth // step

    def kernel(t0, t1, t2, t3, c, c2, out, held):
        @pl.when(pl.program_id(0) == 0)
        def _():
            held[0] = c[...].T
            for j in range(pieces):
                held[1, :, j * part : (j + 1) * part] = c2[j].T

        total = dot(held[0], jnp.concatenate([t0[...], t1[...]], axis=0))
        total = total + dot(held[1], jnp.concatenate([t2[...], t3[...]], axis=0))
        out[...] = total.astype(BF16)

    t_spec = spec((half, step), lambda m: (0, m))
    o_spec = spec((half, step), lambda m: (0, first + m))
    return call(
        kernel,
        (depth // step,),
        [
            t_spec,
            t_spec,
            o_spec,
            o_spec,
            spec((None, seq, width), lambda m: (0, 0, 0)),
            spec((pieces, None, part, width), lambda m: (0, 0, 0, 0)),
        ],
        spec((width, step), lambda m: (0, m)),
        jax.ShapeDtypeStruct((width, depth), BF16),
        4 * seq * depth * width,
        [pltpu.VMEM((2, width, seq), BF16)],
    )(mine, sib, other_mine, other_sib, done, done2)


def after(x, *others):
    return lax.optimization_barrier((x, *others))[0]


def body(tokens, w_qkv, w_out, cotangent):
    n_row = lax.axis_size("row")
    n_col = lax.axis_size("colxdept")
    n_dp = lax.axis_size("dp")
    chips = n_col // 2
    tile = tokens.shape[1]
    seq = tile * n_col
    half, local = seq // 2, seq // n_row
    core = lax.axis_index("colxdept") % 2
    row = lax.axis_index("row").astype(jnp.int32)
    at = row[None]
    same_core = [list(range(c, n_col, 2)) for c in range(2)]

    def swap_cores(x):
        return lax.ppermute(x, "colxdept", [(i, i ^ 1) for i in range(n_col)])

    def swap_dp(x):
        return lax.ppermute(x, "dp", [(i, (i + 1) % n_dp) for i in range(n_dp)])

    def along_row(x, step):
        return lax.ppermute(x, "row", [(i, (i + step) % n_row) for i in range(n_row)])

    def among_chips(x):
        return lax.all_to_all(x, "colxdept", 0, 0, axis_index_groups=same_core)

    def gather_core(x):
        return among_chips(jnp.broadcast_to(x[None], (chips, *x.shape))).reshape(half, -1)

    def gather_row(x):
        return [x] + [along_row(x, -j) for j in range(1, n_row)]

    def sum_row(parts):
        total = parts[0]
        for j in range(1, n_row):
            total = total + along_row(parts[j], j)
        return total.astype(BF16)

    index = jnp.arange(seq, dtype=jnp.int32)
    owner = (index // half + core) % 2
    position = ((index % half) // tile * 2 + owner) * tile + index % tile
    rows, cols = position[:, None], position[None, :]

    w_out_sib = swap_cores(w_out)
    w_qkv_sib = swap_cores(w_qkv)
    tok_mine, w_out_sib, w_qkv_sib = lax.optimization_barrier((gather_core(tokens[0]), w_out_sib, w_qkv_sib))
    tok_sib = swap_cores(tok_mine)
    cot_mine = gather_core(after(cotangent[0], tok_mine))
    qkv_part = project(tok_mine, tok_sib, w_qkv)

    other = swap_dp(after(jnp.concatenate([tokens[0], cotangent[0]], axis=1), tok_mine))
    cot_mine = after(cot_mine, qkv_part)
    cot_sib = swap_cores(cot_mine)
    back_parts = back_context(at, cot_mine, cot_sib, w_out, n_row)
    other_mine = gather_core(after(other, *back_parts))

    qkv_sum = lax.psum_scatter(qkv_part, "row", scatter_dimension=0, tiled=True).astype(BF16)
    pieces = gather_row(qkv_sum)
    back_pieces = gather_row(sum_row(back_parts))
    done = attention(rows, cols, place(at, pieces, back_pieces))
    done_sib = swap_cores(done[:, half:])
    quarter = swap_dp(lax.dynamic_slice_in_dim(done, row * local, local, axis=1))
    done_sib, quarter, other_mine = lax.optimization_barrier((done_sib, quarter, other_mine))
    done2 = lax.all_gather(quarter, "row")
    other_sib = swap_cores(other_mine)
    shares = among_chips(partials(chips, done, done_sib, w_out, w_out_sib, w_qkv, w_qkv_sib))
    grad_out = weight_out(cot_mine, cot_sib, other_mine, other_sib, done, done2)
    grad_qkv = weight_qkv(tok_mine, tok_sib, other_mine, other_sib, done, done2)
    shares = after(shares, grad_out, grad_qkv)
    results = jnp.sum(shares.astype(F32), axis=0).astype(BF16)
    return (results[:1], results[1:], grad_qkv, grad_out)


def solution(mesh):
    return jax.shard_map(
        body,
        mesh=mesh,
        in_specs=(
            P("dp", "colxdept", "row"),
            P(None, "row", "colxdept"),
            P("colxdept", "row"),
            P("dp", "colxdept", "row"),
        ),
        out_specs=(
            P("dp", "colxdept", "row"),
            P("dp", "colxdept", "row"),
            P(None, "row", "colxdept"),
            P("colxdept", "row"),
        ),
        check_vma=False,
    )
```

```python
import jax
import jax.numpy as jnp
from jax import lax
from jax.experimental import pallas as pl
from jax.experimental.pallas import tpu as pltpu
from jax.sharding import PartitionSpec as P

DH = 128
F32 = jnp.float32
BF16 = jnp.bfloat16
NT = (((1,), (1,)), ((), ()))
TN = (((0,), (0,)), ((), ()))
ROOM = 56 * 2**20


def dot(a, b, dims=None):
    if dims is None:
        return jnp.dot(a, b, preferred_element_type=F32)
    return lax.dot_general(a, b, dims, preferred_element_type=F32)


def call(kernel, grid, in_specs, out_specs, out_shape, flops, scratch=(), aliases=None):
    def run(*args):
        many = out_shape if isinstance(out_shape, list) else [out_shape]
        moved = sum(a.size * a.dtype.itemsize for a in [*args, *many])
        return pl.pallas_call(
            kernel,
            grid=grid,
            in_specs=in_specs,
            out_specs=out_specs,
            out_shape=out_shape,
            scratch_shapes=list(scratch),
            input_output_aliases=aliases or {},
            compiler_params=pltpu.CompilerParams(vmem_limit_bytes=ROOM),
            cost_estimate=pl.CostEstimate(flops=flops, bytes_accessed=moved, transcendentals=0),
        )(*args)

    return run


def spec(block, index):
    return pl.BlockSpec(block, index)


def whole(x):
    return pl.BlockSpec(x.shape, lambda *_: (0,) * x.ndim)


SCALAR = pl.BlockSpec(memory_space=pltpu.SMEM)


def nth_part(row, j, n, part):
    return pl.ds(pl.multiple_of((row[0] + j) % n * part, part), part)


def project(mine, sib, w):
    n, depth, width = w.shape
    half = mine.shape[0]

    def kernel(mine, sib, w, out):
        out[:half] = dot(mine[...], w[...])
        out[half:] = dot(sib[...], w[...])

    return call(
        kernel,
        (n,),
        [whole(mine), whole(sib), spec((None, depth, width), lambda a: (a, 0, 0))],
        spec((2 * half, width), lambda a: (0, a)),
        jax.ShapeDtypeStruct((2 * half, n * width), F32),
        4 * half * n * depth * width,
    )(mine, sib, w)


def back_context(row, mine, sib, w, n_row):
    width, depth = w.shape
    half = mine.shape[0]
    part = 2 * half // n_row

    def kernel(row, mine, sib, w, *rest):
        outs, total = rest[:-1], rest[-1]

        @pl.when(pl.program_id(0) == 0)
        def _():
            total[...] = jnp.zeros_like(total)

        total[:half] += dot(mine[...], w[...], NT)
        total[half:] += dot(sib[...], w[...], NT)

        @pl.when(pl.program_id(0) == pl.num_programs(0) - 1)
        def _():
            for j, out in enumerate(outs):
                out[...] = total[nth_part(row, j, n_row, part)]

    step = min(1024, depth)
    x_spec = spec((half, step), lambda k: (0, k))
    return call(
        kernel,
        (depth // step,),
        [SCALAR, x_spec, x_spec, spec((width, step), lambda k: (0, k))],
        [spec((part, width), lambda k: (0, 0))] * n_row,
        [jax.ShapeDtypeStruct((part, width), F32)] * n_row,
        4 * half * depth * width,
        [pltpu.VMEM((2 * half, width), F32)],
    )(row, mine, sib, w)


def place(row, left, right):
    n = len(left)
    part, split = left[0].shape
    shape = (n * part, split + right[0].shape[1])

    def kernel(row, *refs):
        out = refs[-1]
        for j in range(n):
            rows = nth_part(row, j, n, part)
            out[rows, :split] = refs[j][...]
            out[rows, split:] = refs[n + j][...]

    flat = [*left, *right]
    return call(
        kernel,
        (1,),
        [SCALAR] + [whole(x) for x in flat],
        spec(shape, lambda _: (0, 0)),
        jax.ShapeDtypeStruct(shape, BF16),
        0,
    )(row, *flat)


def attention(row, rows, cols, held, n_row):
    seq, width = held.shape[0], held.shape[1] // 4
    half, part = seq // 2, seq // n_row
    heads = width // DH
    scale = 1.0 / DH**0.5

    def kernel(row, rows, cols, q, k, v, g, out, out_sib, out_part):
        scores = dot(q[...], k[...], NT) * scale
        scores = jnp.where(rows[...] >= cols[...], scores, -1e30)
        expo = jnp.exp(scores - jnp.max(scores, axis=-1, keepdims=True))
        probs = expo / jnp.sum(expo, axis=-1, keepdims=True)
        probs_b = probs.astype(BF16)
        out[0] = dot(probs_b, v[...]).astype(BF16)
        out[3] = dot(probs_b, g[...], TN).astype(BF16)
        grad_probs = dot(g[...], v[...], NT)
        delta = jnp.sum(grad_probs * probs, axis=-1, keepdims=True)
        grad_scores = (probs * (grad_probs - delta) * scale).astype(BF16)
        out[1] = dot(grad_scores, k[...]).astype(BF16)
        out[2] = dot(grad_scores, q[...], TN).astype(BF16)
        out_sib[...] = out[:, half:]
        out_part[...] = out[:, nth_part(row, 0, n_row, part)]

    def head(a):
        return spec((seq, DH), lambda h: (0, a * heads + h))

    return call(
        kernel,
        (heads,),
        [SCALAR, whole(rows), whole(cols)] + [head(a) for a in range(4)],
        [spec((4, n, DH), lambda h: (0, 0, h)) for n in (seq, half, part)],
        [jax.ShapeDtypeStruct((4, n, width), BF16) for n in (seq, half, part)],
        14 * heads * seq * seq * DH,
    )(row, rows, cols, held, held, held, held)


def mix(chips, done, done_sib, w, w_sib):
    width, depth = w.shape
    half = done_sib.shape[1]
    step = min(1024, depth)

    def kernel(d, ds, w, ws, out):
        out[...] = (dot(d[...], w[...]) + dot(ds[...], ws[...])).astype(BF16).reshape(out.shape)

    d_spec = spec((None, half, width), lambda m: (0, 0, 0))
    w_spec = spec((width, step), lambda m: (0, m))
    return call(
        kernel,
        (depth // step,),
        [d_spec, d_spec, w_spec, w_spec],
        spec((chips, None, half // chips, step), lambda m: (0, 0, 0, m)),
        jax.ShapeDtypeStruct((chips, 2, half // chips, depth), BF16),
        4 * half * depth * width,
    )(done, done_sib, w, w_sib)


def back_tokens(first, done, done_sib, w, w_sib):
    n, depth, width = w.shape
    chips, half = first.shape[0], done_sib.shape[1]
    step = min(512, depth)

    def side(x, start):
        return [x[a] for a in range(start, n + start)]

    def kernel(_, d, ds, w, ws, out):
        grads = jnp.concatenate(side(d, 1) + side(ds, 1), axis=1)
        weights = jnp.concatenate(side(w, 0) + side(ws, 0), axis=1)
        out[...] = dot(grads, weights, NT).astype(BF16).reshape(out.shape)

    d_spec = spec((n + 1, half, width), lambda m: (0, 0, 0))
    w_spec = spec((n, step, width), lambda m: (0, m, 0))
    return call(
        kernel,
        (depth // step,),
        [pl.BlockSpec(memory_space=pl.ANY), d_spec, d_spec, w_spec, w_spec],
        spec((chips, None, half // chips, step), lambda m: (0, 1, 0, m)),
        jax.ShapeDtypeStruct(first.shape, BF16),
        4 * half * n * depth * width,
        aliases={0: 0},
    )(first, done, done_sib, w, w_sib)


def weight_qkv(mine, sib, other_mine, other_sib, done, done2):
    n, seq, width = done.shape[0] - 1, *done.shape[1:]
    half, depth = mine.shape
    pieces, part = done2.shape[0], done2.shape[2]
    step = min(1024, depth)

    def kernel(t0, t1, t2, t3, d, d2, out, held):
        @pl.when(pl.program_id(0) == 0)
        def _():
            for a in range(n):
                columns = slice(a * width, (a + 1) * width)
                held[0, :, columns] = d[a + 1]
                for j in range(pieces):
                    held[1, j * part : (j + 1) * part, columns] = d2[j, a + 1]

        x = jnp.concatenate([t0[...], t1[...], t2[...], t3[...]], axis=0)
        total = dot(x, held[...].reshape(2 * seq, n * width), TN)
        for a in range(n):
            out[a] = total[:, a * width : (a + 1) * width].astype(BF16)

    t_spec = spec((half, step), lambda m: (0, m))
    return call(
        kernel,
        (depth // step,),
        [t_spec] * 4 + [whole(done), whole(done2)],
        spec((n, step, width), lambda m: (0, m, 0)),
        jax.ShapeDtypeStruct((n, depth, width), BF16),
        4 * seq * n * depth * width,
        [pltpu.VMEM((2, seq, n * width), BF16)],
    )(mine, sib, other_mine, other_sib, done, done2)


def weight_out(mine, sib, other_mine, other_sib, done, done2):
    seq, width = done.shape[1:]
    half, depth = mine.shape
    pieces, part = done2.shape[0], done2.shape[2]
    step = min(1024, depth)
    first = depth // step

    def kernel(t0, t1, t2, t3, c, c2, out, held):
        @pl.when(pl.program_id(0) == 0)
        def _():
            held[0] = c[...].T
            for j in range(pieces):
                held[1, :, j * part : (j + 1) * part] = c2[j].T

        total = dot(held[0], jnp.concatenate([t0[...], t1[...]], axis=0))
        total = total + dot(held[1], jnp.concatenate([t2[...], t3[...]], axis=0))
        out[...] = total.astype(BF16)

    t_spec = spec((half, step), lambda m: (0, m))
    o_spec = spec((half, step), lambda m: (0, first + m))
    return call(
        kernel,
        (depth // step,),
        [
            t_spec,
            t_spec,
            o_spec,
            o_spec,
            spec((None, seq, width), lambda m: (0, 0, 0)),
            spec((pieces, None, part, width), lambda m: (0, 0, 0, 0)),
        ],
        spec((width, step), lambda m: (0, m)),
        jax.ShapeDtypeStruct((width, depth), BF16),
        4 * seq * depth * width,
        [pltpu.VMEM((2, width, seq), BF16)],
    )(mine, sib, other_mine, other_sib, done, done2)


def after(x, *others):
    return lax.optimization_barrier((x, *others))[0]


def body(tokens, w_qkv, w_out, cotangent):
    n_row = lax.axis_size("row")
    n_col = lax.axis_size("colxdept")
    n_dp = lax.axis_size("dp")
    chips = n_col // 2
    tile = tokens.shape[1]
    seq = tile * n_col
    half, local = seq // 2, seq // n_row
    core = lax.axis_index("colxdept") % 2
    row = lax.axis_index("row").astype(jnp.int32)
    at = row[None]
    same_core = [list(range(c, n_col, 2)) for c in range(2)]

    def swap_cores(x):
        return lax.ppermute(x, "colxdept", [(i, i ^ 1) for i in range(n_col)])

    def swap_dp(x):
        return lax.ppermute(x, "dp", [(i, (i + 1) % n_dp) for i in range(n_dp)])

    def along_row(x, step):
        return lax.ppermute(x, "row", [(i, (i + step) % n_row) for i in range(n_row)])

    def among_chips(x):
        return lax.all_to_all(x, "colxdept", 0, 0, axis_index_groups=same_core)

    def gather_core(x):
        return among_chips(jnp.broadcast_to(x[None], (chips, *x.shape))).reshape(half, -1)

    def gather_row(x):
        return [x] + [along_row(x, -j) for j in range(1, n_row)]

    index = jnp.arange(seq, dtype=jnp.int32)
    owner = (index // half + core) % 2
    position = ((index % half) // tile * 2 + owner) * tile + index % tile
    rows, cols = position[:, None], position[None, :]

    w_out_sib = swap_cores(w_out)
    w_qkv_sib = swap_cores(w_qkv)
    tok_mine, w_out_sib, w_qkv_sib = lax.optimization_barrier((gather_core(tokens[0]), w_out_sib, w_qkv_sib))
    tok_sib = swap_cores(tok_mine)
    other = swap_dp(after(jnp.concatenate([tokens[0], cotangent[0]], axis=1), tok_mine))
    qkv_part = project(tok_mine, tok_sib, w_qkv)
    cot_mine = after(gather_core(after(cotangent[0], tok_mine)), qkv_part, other)
    cot_sib = swap_cores(cot_mine)
    other_mine = gather_core(after(other, cot_mine))
    back_parts = back_context(at, cot_mine, cot_sib, w_out, n_row)

    qkv_sum = lax.psum_scatter(qkv_part, "row", scatter_dimension=0, tiled=True).astype(BF16)
    pieces = gather_row(qkv_sum)
    arrived = [back_parts[0]] + [along_row(back_parts[j], j) for j in range(1, n_row)]
    back_pieces = gather_row(sum(arrived[1:], arrived[0]).astype(BF16))

    done, second, quarter = attention(at, rows, cols, place(at, pieces, back_pieces), n_row)
    quarter = swap_dp(quarter)
    done_sib = swap_cores(second)
    first = mix(chips, done, done_sib, w_out, w_out_sib)
    first, quarter, other_mine = lax.optimization_barrier((first, quarter, other_mine))
    done2 = lax.all_gather(quarter, "row")
    other_sib = swap_cores(other_mine)
    shares = among_chips(back_tokens(first, done, done_sib, w_qkv, w_qkv_sib))
    grad_out = weight_out(cot_mine, cot_sib, other_mine, other_sib, done, done2)
    grad_qkv = weight_qkv(tok_mine, tok_sib, other_mine, other_sib, done, done2)
    shares = after(shares, grad_out, grad_qkv)
    results = jnp.sum(shares.astype(F32), axis=0).astype(BF16)
    return (results[:1], results[1:], grad_qkv, grad_out)


def solution(mesh):
    return jax.shard_map(
        body,
        mesh=mesh,
        in_specs=(
            P("dp", "colxdept", "row"),
            P(None, "row", "colxdept"),
            P("colxdept", "row"),
            P("dp", "colxdept", "row"),
        ),
        out_specs=(
            P("dp", "colxdept", "row"),
            P("dp", "colxdept", "row"),
            P(None, "row", "colxdept"),
            P("colxdept", "row"),
        ),
        check_vma=False,
    )
```

```python
import jax
import jax.numpy as jnp
from jax import lax
from jax.experimental import pallas as pl
from jax.experimental.pallas import tpu as pltpu
from jax.sharding import PartitionSpec as P

DH = 128
F32 = jnp.float32
BF16 = jnp.bfloat16
NT = (((1,), (1,)), ((), ()))
TN = (((0,), (0,)), ((), ()))
ROOM = 56 * 2**20


def dot(a, b, dims=None):
    if dims is None:
        return jnp.dot(a, b, preferred_element_type=F32)
    return lax.dot_general(a, b, dims, preferred_element_type=F32)


def call(kernel, grid, in_specs, out_specs, out_shape, flops, scratch=()):
    def run(*args):
        many = out_shape if isinstance(out_shape, list) else [out_shape]
        moved = sum(a.size * a.dtype.itemsize for a in [*args, *many])
        return pl.pallas_call(
            kernel,
            grid=grid,
            in_specs=in_specs,
            out_specs=out_specs,
            out_shape=out_shape,
            scratch_shapes=list(scratch),
            compiler_params=pltpu.CompilerParams(vmem_limit_bytes=ROOM),
            cost_estimate=pl.CostEstimate(flops=flops, bytes_accessed=moved, transcendentals=0),
        )(*args)

    return run


def spec(block, index):
    return pl.BlockSpec(block, index)


def whole(x):
    return pl.BlockSpec(x.shape, lambda *_: (0,) * x.ndim)


SCALAR = pl.BlockSpec(memory_space=pltpu.SMEM)


def nth_part(row, j, n, part):
    return pl.ds(pl.multiple_of((row[0] + j) % n * part, part), part)


def project(row, mine, sib, w, n_row):
    n, depth, width = w.shape
    half = mine.shape[0]
    part = 2 * half // n_row

    def kernel(row, mine, sib, w, *rest):
        outs, held = rest[:-1], rest[-1]

        @pl.when(pl.program_id(0) == 0)
        def _():
            held[:half] = mine[...]
            held[half:] = sib[...]

        for j, out in enumerate(outs):
            out[...] = dot(held[nth_part(row, j, n_row, part)], w[...])

    return call(
        kernel,
        (n,),
        [SCALAR, whole(mine), whole(sib), spec((None, depth, width), lambda a: (a, 0, 0))],
        [spec((part, width), lambda a: (0, a))] * n_row,
        [jax.ShapeDtypeStruct((part, n * width), F32)] * n_row,
        4 * half * n * depth * width,
        [pltpu.VMEM((2 * half, depth), BF16)],
    )(row, mine, sib, w)


def back_context(row, mine, sib, w, n_row):
    width, depth = w.shape
    half = mine.shape[0]
    part = 2 * half // n_row

    def kernel(row, mine, sib, w, *rest):
        outs, total = rest[:-1], rest[-1]

        @pl.when(pl.program_id(0) == 0)
        def _():
            total[...] = jnp.zeros_like(total)

        total[:half] += dot(mine[...], w[...], NT)
        total[half:] += dot(sib[...], w[...], NT)

        @pl.when(pl.program_id(0) == pl.num_programs(0) - 1)
        def _():
            for j, out in enumerate(outs):
                out[...] = total[nth_part(row, j, n_row, part)]

    step = min(1024, depth)
    x_spec = spec((half, step), lambda k: (0, k))
    return call(
        kernel,
        (depth // step,),
        [SCALAR, x_spec, x_spec, spec((width, step), lambda k: (0, k))],
        [spec((part, width), lambda k: (0, 0))] * n_row,
        [jax.ShapeDtypeStruct((part, width), F32)] * n_row,
        4 * half * depth * width,
        [pltpu.VMEM((2 * half, width), F32)],
    )(row, mine, sib, w)


def place(row, left, right):
    n = len(left)
    part, split = left[0].shape
    shape = (n * part, split + right[0].shape[1])

    def kernel(row, *refs):
        out = refs[-1]
        for j in range(n):
            rows = nth_part(row, j, n, part)
            out[rows, :split] = refs[j][...]
            out[rows, split:] = refs[n + j][...]

    flat = [*left, *right]
    return call(
        kernel,
        (1,),
        [SCALAR] + [whole(x) for x in flat],
        spec(shape, lambda _: (0, 0)),
        jax.ShapeDtypeStruct(shape, BF16),
        0,
    )(row, *flat)


def attention(row, rows, cols, held, n_row):
    seq, width = held.shape[0], held.shape[1] // 4
    half, part = seq // 2, seq // n_row
    heads = width // DH
    scale = 1.0 / DH**0.5

    def kernel(row, rows, cols, q, k, v, g, out, out_sib, out_part):
        scores = dot(q[...], k[...], NT) * scale
        scores = jnp.where(rows[...] >= cols[...], scores, -1e30)
        expo = jnp.exp(scores - jnp.max(scores, axis=-1, keepdims=True))
        probs = expo / jnp.sum(expo, axis=-1, keepdims=True)
        probs_b = probs.astype(BF16)
        out[0] = dot(probs_b, v[...]).astype(BF16)
        out[3] = dot(probs_b, g[...], TN).astype(BF16)
        grad_probs = dot(g[...], v[...], NT)
        delta = jnp.sum(grad_probs * probs, axis=-1, keepdims=True)
        grad_scores = (probs * (grad_probs - delta) * scale).astype(BF16)
        out[1] = dot(grad_scores, k[...]).astype(BF16)
        out[2] = dot(grad_scores, q[...], TN).astype(BF16)
        out_sib[...] = out[:, half:]
        out_part[...] = out[:, nth_part(row, 0, n_row, part)]

    def head(a):
        return spec((seq, DH), lambda h: (0, a * heads + h))

    return call(
        kernel,
        (heads,),
        [SCALAR, whole(rows), whole(cols)] + [head(a) for a in range(4)],
        [spec((4, n, DH), lambda h: (0, 0, h)) for n in (seq, half, part)],
        [jax.ShapeDtypeStruct((4, n, width), BF16) for n in (seq, half, part)],
        14 * heads * seq * seq * DH,
    )(row, rows, cols, held, held, held, held)


def mix(chips, context, context_sib, w, w_sib):
    width, depth = w.shape
    half = context_sib.shape[1]
    step = min(1024, depth)

    def kernel(c, cs, w, ws, out):
        out[...] = (dot(c[...], w[...]) + dot(cs[...], ws[...])).astype(BF16).reshape(out.shape)

    c_spec = spec((None, half, width), lambda m: (0, 0, 0))
    w_spec = spec((width, step), lambda m: (0, m))
    return call(
        kernel,
        (depth // step,),
        [c_spec, c_spec, w_spec, w_spec],
        spec((chips, half // chips, step), lambda m: (0, 0, m)),
        jax.ShapeDtypeStruct((chips, half // chips, depth), BF16),
        4 * half * depth * width,
    )(context, context_sib, w, w_sib)


def back_tokens(chips, grads, grads_sib, w, w_sib):
    n, depth, width = w.shape
    half = grads_sib.shape[1]
    step = min(512, depth)

    def kernel(g, gs, w, ws, out):
        grads = jnp.concatenate([x[a + 1] for x in (g, gs) for a in range(n)], axis=1)
        weights = jnp.concatenate([x[a] for x in (w, ws) for a in range(n)], axis=1)
        out[...] = dot(grads, weights, NT).astype(BF16).reshape(out.shape)

    g_spec = spec((n + 1, half, width), lambda m: (0, 0, 0))
    w_spec = spec((n, step, width), lambda m: (0, m, 0))
    return call(
        kernel,
        (depth // step,),
        [g_spec, g_spec, w_spec, w_spec],
        spec((chips, half // chips, step), lambda m: (0, 0, m)),
        jax.ShapeDtypeStruct((chips, half // chips, depth), BF16),
        4 * half * n * depth * width,
    )(grads, grads_sib, w, w_sib)


def weight_qkv(row, mine, sib, other_mine, other_sib, done, done2):
    n, seq, width = done.shape[0] - 1, *done.shape[1:]
    half, depth = mine.shape
    pieces, part = len(done2), done2[0].shape[1]
    step = min(1024, depth)

    def kernel(row, t0, t1, t2, t3, d, *rest):
        d2, out, held = rest[:pieces], rest[-2], rest[-1]

        @pl.when(pl.program_id(0) == 0)
        def _():
            for a in range(n):
                columns = slice(a * width, (a + 1) * width)
                held[0, :, columns] = d[a + 1]
                for j in range(pieces):
                    held[1, nth_part(row, j, pieces, part), columns] = d2[j][a + 1]

        x = jnp.concatenate([t0[...], t1[...], t2[...], t3[...]], axis=0)
        total = dot(x, held[...].reshape(2 * seq, n * width), TN)
        for a in range(n):
            out[a] = total[:, a * width : (a + 1) * width].astype(BF16)

    t_spec = spec((half, step), lambda m: (0, m))
    return call(
        kernel,
        (depth // step,),
        [SCALAR] + [t_spec] * 4 + [whole(done)] + [whole(x) for x in done2],
        spec((n, step, width), lambda m: (0, m, 0)),
        jax.ShapeDtypeStruct((n, depth, width), BF16),
        4 * seq * n * depth * width,
        [pltpu.VMEM((2, seq, n * width), BF16)],
    )(row, mine, sib, other_mine, other_sib, done, *done2)


def weight_out(row, mine, sib, other_mine, other_sib, done, done2):
    seq, width = done.shape[1:]
    half, depth = mine.shape
    pieces, part = len(done2), done2[0].shape[1]
    step = min(1024, depth)
    first = depth // step

    def kernel(row, t0, t1, t2, t3, c, *rest):
        c2, out, held = rest[:pieces], rest[-2], rest[-1]

        @pl.when(pl.program_id(0) == 0)
        def _():
            held[0] = c[...].T
            for j in range(pieces):
                held[1, :, nth_part(row, j, pieces, part)] = c2[j][...].T

        total = dot(held[0], jnp.concatenate([t0[...], t1[...]], axis=0))
        total = total + dot(held[1], jnp.concatenate([t2[...], t3[...]], axis=0))
        out[...] = total.astype(BF16)

    t_spec = spec((half, step), lambda m: (0, m))
    o_spec = spec((half, step), lambda m: (0, first + m))
    return call(
        kernel,
        (depth // step,),
        [SCALAR, t_spec, t_spec, o_spec, o_spec, spec((None, seq, width), lambda m: (0, 0, 0))]
        + [spec((None, part, width), lambda m: (0, 0, 0))] * pieces,
        spec((width, step), lambda m: (0, m)),
        jax.ShapeDtypeStruct((width, depth), BF16),
        4 * seq * depth * width,
        [pltpu.VMEM((2, width, seq), BF16)],
    )(row, mine, sib, other_mine, other_sib, done, *done2)


def after(x, *others):
    return lax.optimization_barrier((x, *others))[0]


def body(tokens, w_qkv, w_out, cotangent):
    n_row = lax.axis_size("row")
    n_col = lax.axis_size("colxdept")
    n_dp = lax.axis_size("dp")
    chips = n_col // 2
    tile = tokens.shape[1]
    seq = tile * n_col
    half, local = seq // 2, seq // n_row
    core = lax.axis_index("colxdept") % 2
    row = lax.axis_index("row").astype(jnp.int32)
    at = row[None]
    same_core = [list(range(c, n_col, 2)) for c in range(2)]

    def swap_cores(x):
        return lax.ppermute(x, "colxdept", [(i, i ^ 1) for i in range(n_col)])

    def swap_dp(x):
        return lax.ppermute(x, "dp", [(i, (i + 1) % n_dp) for i in range(n_dp)])

    def along_row(x, step):
        return lax.ppermute(x, "row", [(i, (i + step) % n_row) for i in range(n_row)])

    def among_chips(x):
        return lax.all_to_all(x, "colxdept", 0, 0, axis_index_groups=same_core)

    def gather_core(x):
        return among_chips(jnp.broadcast_to(x[None], (chips, *x.shape))).reshape(half, -1)

    def gather_row(x):
        return [x] + [along_row(x, -j) for j in range(1, n_row)]

    def sum_row(parts):
        total = parts[0]
        for j in range(1, n_row):
            total = total + along_row(parts[j], j)
        return total.astype(BF16)

    index = jnp.arange(seq, dtype=jnp.int32)
    owner = (index // half + core) % 2
    position = ((index % half) // tile * 2 + owner) * tile + index % tile
    rows, cols = position[:, None], position[None, :]

    w_out_sib = swap_cores(w_out)
    w_qkv_sib = swap_cores(w_qkv)
    tok_mine, w_out_sib, w_qkv_sib = lax.optimization_barrier((gather_core(tokens[0]), w_out_sib, w_qkv_sib))
    tok_sib = swap_cores(tok_mine)
    other = swap_dp(after(jnp.concatenate([tokens[0], cotangent[0]], axis=1), tok_mine))
    qkv_parts = project(at, tok_mine, tok_sib, w_qkv, n_row)
    cot_mine = gather_core(after(cotangent[0], other, *qkv_parts))
    other_mine = gather_core(after(other, cot_mine))
    qkv_sum = sum_row(qkv_parts)
    pieces = gather_row(qkv_sum)
    cot_mine = after(cot_mine, qkv_sum)
    cot_sib = after(swap_cores(cot_mine), pieces[1], pieces[3])
    back_parts = back_context(at, cot_mine, cot_sib, w_out, n_row)
    back_pieces = gather_row(sum_row(back_parts))

    done, second, quarter = attention(at, rows, cols, place(at, pieces, back_pieces), n_row)
    quarter = swap_dp(quarter)
    done_sib = swap_cores(second)
    mix_part = after(mix(chips, done, done_sib, w_out, w_out_sib), other_mine, quarter)
    mix_shares = among_chips(mix_part)
    other_sib = swap_cores(after(other_mine, mix_part))
    done2 = gather_row(quarter)
    back_part = back_tokens(chips, done, after(done_sib, mix_part, quarter), w_qkv, w_qkv_sib)
    mixed = jnp.sum(after(mix_shares, back_part, *done2).astype(F32), axis=0).astype(BF16)
    back_shares = among_chips(after(back_part, mixed))
    grad_out = weight_out(at, cot_mine, cot_sib, other_mine, other_sib, done, done2)
    grad_qkv = weight_qkv(at, tok_mine, tok_sib, other_mine, other_sib, done, done2)
    back_shares = after(back_shares, grad_out, grad_qkv)
    grad_tokens = jnp.sum(back_shares.astype(F32), axis=0).astype(BF16)
    return (mixed[None], grad_tokens[None], grad_qkv, grad_out)


def solution(mesh):
    return jax.shard_map(
        body,
        mesh=mesh,
        in_specs=(
            P("dp", "colxdept", "row"),
            P(None, "row", "colxdept"),
            P("colxdept", "row"),
            P("dp", "colxdept", "row"),
        ),
        out_specs=(
            P("dp", "colxdept", "row"),
            P("dp", "colxdept", "row"),
            P(None, "row", "colxdept"),
            P("colxdept", "row"),
        ),
        check_vma=False,
    )
```

```python
import jax
import jax.numpy as jnp
from jax import lax
from jax.experimental import pallas as pl
from jax.experimental.pallas import tpu as pltpu
from jax.sharding import PartitionSpec as P

DH = 128
F32 = jnp.float32
BF16 = jnp.bfloat16
NT = (((1,), (1,)), ((), ()))
TN = (((0,), (0,)), ((), ()))
ROOM = 56 * 2**20


def dot(a, b, dims=None):
    if dims is None:
        return jnp.dot(a, b, preferred_element_type=F32)
    return lax.dot_general(a, b, dims, preferred_element_type=F32)


def call(kernel, grid, in_specs, out_specs, out_shape, flops, scratch=()):
    def run(*args):
        many = out_shape if isinstance(out_shape, list) else [out_shape]
        moved = sum(a.size * a.dtype.itemsize for a in [*args, *many])
        return pl.pallas_call(
            kernel,
            grid=grid,
            in_specs=in_specs,
            out_specs=out_specs,
            out_shape=out_shape,
            scratch_shapes=list(scratch),
            compiler_params=pltpu.CompilerParams(vmem_limit_bytes=ROOM),
            cost_estimate=pl.CostEstimate(flops=flops, bytes_accessed=moved, transcendentals=0),
        )(*args)

    return run


def spec(block, index):
    return pl.BlockSpec(block, index)


def whole(x):
    return pl.BlockSpec(x.shape, lambda *_: (0,) * x.ndim)


SCALAR = pl.BlockSpec(memory_space=pltpu.SMEM)


def nth_part(row, j, n, part):
    return pl.ds(pl.multiple_of((row[0] + j) % n * part, part), part)


def project(row, mine, sib, w, n_row):
    n, depth, width = w.shape
    half = mine.shape[0]
    part = 2 * half // n_row

    def kernel(row, mine, sib, w, *rest):
        outs, held = rest[:-1], rest[-1]

        @pl.when(pl.program_id(0) == 0)
        def _():
            held[:half] = mine[...]
            held[half:] = sib[...]

        for j, out in enumerate(outs):
            out[...] = dot(held[nth_part(row, j, n_row, part)], w[...])

    return call(
        kernel,
        (n,),
        [SCALAR, whole(mine), whole(sib), spec((None, depth, width), lambda a: (a, 0, 0))],
        [spec((part, width), lambda a: (0, a))] * n_row,
        [jax.ShapeDtypeStruct((part, n * width), F32)] * n_row,
        4 * half * n * depth * width,
        [pltpu.VMEM((2 * half, depth), BF16)],
    )(row, mine, sib, w)


def back_context(row, mine, sib, w, n_row):
    width, depth = w.shape
    half = mine.shape[0]
    part = 2 * half // n_row

    def kernel(row, mine, sib, w, *rest):
        outs, total = rest[:-1], rest[-1]

        @pl.when(pl.program_id(0) == 0)
        def _():
            total[...] = jnp.zeros_like(total)

        total[:half] += dot(mine[...], w[...], NT)
        total[half:] += dot(sib[...], w[...], NT)

        @pl.when(pl.program_id(0) == pl.num_programs(0) - 1)
        def _():
            for j, out in enumerate(outs):
                out[...] = total[nth_part(row, j, n_row, part)]

    step = min(1024, depth)
    x_spec = spec((half, step), lambda k: (0, k))
    return call(
        kernel,
        (depth // step,),
        [SCALAR, x_spec, x_spec, spec((width, step), lambda k: (0, k))],
        [spec((part, width), lambda k: (0, 0))] * n_row,
        [jax.ShapeDtypeStruct((part, width), F32)] * n_row,
        4 * half * depth * width,
        [pltpu.VMEM((2 * half, width), F32)],
    )(row, mine, sib, w)


def place(row, left, right):
    n = len(left)
    part, split = left[0].shape
    shape = (n * part, split + right[0].shape[1])

    def kernel(row, *refs):
        out = refs[-1]
        for j in range(n):
            rows = nth_part(row, j, n, part)
            out[rows, :split] = refs[j][...]
            out[rows, split:] = refs[n + j][...]

    flat = [*left, *right]
    return call(
        kernel,
        (1,),
        [SCALAR] + [whole(x) for x in flat],
        spec(shape, lambda _: (0, 0)),
        jax.ShapeDtypeStruct(shape, BF16),
        0,
    )(row, *flat)


def attention(row, rows, cols, held, n_row):
    seq, width = held.shape[0], held.shape[1] // 4
    half, part = seq // 2, seq // n_row
    heads = width // DH
    scale = 1.0 / DH**0.5

    def kernel(row, rows, cols, q, k, v, g, out, out_sib, out_part):
        scores = dot(q[...], k[...], NT) * scale
        scores = jnp.where(rows[...] >= cols[...], scores, -1e30)
        expo = jnp.exp(scores - jnp.max(scores, axis=-1, keepdims=True))
        probs = expo / jnp.sum(expo, axis=-1, keepdims=True)
        probs_b = probs.astype(BF16)
        out[0] = dot(probs_b, v[...]).astype(BF16)
        out[3] = dot(probs_b, g[...], TN).astype(BF16)
        grad_probs = dot(g[...], v[...], NT)
        delta = jnp.sum(grad_probs * probs, axis=-1, keepdims=True)
        grad_scores = (probs * (grad_probs - delta) * scale).astype(BF16)
        out[1] = dot(grad_scores, k[...]).astype(BF16)
        out[2] = dot(grad_scores, q[...], TN).astype(BF16)
        out_sib[...] = out[:, half:]
        out_part[...] = out[:, nth_part(row, 0, n_row, part)]

    def head(a):
        return spec((seq, DH), lambda h: (0, a * heads + h))

    return call(
        kernel,
        (heads,),
        [SCALAR, whole(rows), whole(cols)] + [head(a) for a in range(4)],
        [spec((4, n, DH), lambda h: (0, 0, h)) for n in (seq, half, part)],
        [jax.ShapeDtypeStruct((4, n, width), BF16) for n in (seq, half, part)],
        14 * heads * seq * seq * DH,
    )(row, rows, cols, held, held, held, held)


def mix(chips, context, context_sib, w, w_sib):
    width, depth = w.shape
    half = context_sib.shape[1]
    step = min(1024, depth)

    def kernel(c, cs, w, ws, out):
        out[...] = (dot(c[...], w[...]) + dot(cs[...], ws[...])).astype(BF16).reshape(out.shape)

    c_spec = spec((None, half, width), lambda m: (0, 0, 0))
    w_spec = spec((width, step), lambda m: (0, m))
    return call(
        kernel,
        (depth // step,),
        [c_spec, c_spec, w_spec, w_spec],
        spec((chips, half // chips, step), lambda m: (0, 0, m)),
        jax.ShapeDtypeStruct((chips, half // chips, depth), BF16),
        4 * half * depth * width,
    )(context, context_sib, w, w_sib)


def back_tokens(chips, grads, grads_sib, w, w_sib):
    n, depth, width = w.shape
    half = grads_sib.shape[1]
    step = min(512, depth)

    def kernel(g, gs, w, ws, out):
        grads = jnp.concatenate([x[a + 1] for x in (g, gs) for a in range(n)], axis=1)
        weights = jnp.concatenate([x[a] for x in (w, ws) for a in range(n)], axis=1)
        out[...] = dot(grads, weights, NT).astype(BF16).reshape(out.shape)

    g_spec = spec((n + 1, half, width), lambda m: (0, 0, 0))
    w_spec = spec((n, step, width), lambda m: (0, m, 0))
    return call(
        kernel,
        (depth // step,),
        [g_spec, g_spec, w_spec, w_spec],
        spec((chips, half // chips, step), lambda m: (0, 0, m)),
        jax.ShapeDtypeStruct((chips, half // chips, depth), BF16),
        4 * half * n * depth * width,
    )(grads, grads_sib, w, w_sib)


def weight_qkv(row, mine, sib, other_mine, other_sib, done, done2):
    n, seq, width = done.shape[0] - 1, *done.shape[1:]
    half, depth = mine.shape
    pieces, part = len(done2), done2[0].shape[1]
    step = min(1024, depth)

    def kernel(row, t0, t1, t2, t3, d, *rest):
        d2, out, held = rest[:pieces], rest[-2], rest[-1]

        @pl.when(pl.program_id(0) == 0)
        def _():
            for a in range(n):
                columns = slice(a * width, (a + 1) * width)
                held[0, :, columns] = d[a + 1]
                for j in range(pieces):
                    held[1, nth_part(row, j, pieces, part), columns] = d2[j][a + 1]

        x = jnp.concatenate([t0[...], t1[...], t2[...], t3[...]], axis=0)
        total = dot(x, held[...].reshape(2 * seq, n * width), TN)
        for a in range(n):
            out[a] = total[:, a * width : (a + 1) * width].astype(BF16)

    t_spec = spec((half, step), lambda m: (0, m))
    return call(
        kernel,
        (depth // step,),
        [SCALAR] + [t_spec] * 4 + [whole(done)] + [whole(x) for x in done2],
        spec((n, step, width), lambda m: (0, m, 0)),
        jax.ShapeDtypeStruct((n, depth, width), BF16),
        4 * seq * n * depth * width,
        [pltpu.VMEM((2, seq, n * width), BF16)],
    )(row, mine, sib, other_mine, other_sib, done, *done2)


def weight_out(row, mine, sib, other_mine, other_sib, done, done2):
    seq, width = done.shape[1:]
    half, depth = mine.shape
    pieces, part = len(done2), done2[0].shape[1]
    step = min(1024, depth)
    first = depth // step

    def kernel(row, t0, t1, t2, t3, c, *rest):
        c2, out, held = rest[:pieces], rest[-2], rest[-1]

        @pl.when(pl.program_id(0) == 0)
        def _():
            held[0] = c[...].T
            for j in range(pieces):
                held[1, :, nth_part(row, j, pieces, part)] = c2[j][...].T

        total = dot(held[0], jnp.concatenate([t0[...], t1[...]], axis=0))
        total = total + dot(held[1], jnp.concatenate([t2[...], t3[...]], axis=0))
        out[...] = total.astype(BF16)

    t_spec = spec((half, step), lambda m: (0, m))
    o_spec = spec((half, step), lambda m: (0, first + m))
    return call(
        kernel,
        (depth // step,),
        [SCALAR, t_spec, t_spec, o_spec, o_spec, spec((None, seq, width), lambda m: (0, 0, 0))]
        + [spec((None, part, width), lambda m: (0, 0, 0))] * pieces,
        spec((width, step), lambda m: (0, m)),
        jax.ShapeDtypeStruct((width, depth), BF16),
        4 * seq * depth * width,
        [pltpu.VMEM((2, width, seq), BF16)],
    )(row, mine, sib, other_mine, other_sib, done, *done2)


def after(x, *others):
    return lax.optimization_barrier((x, *others))[0]


def body(tokens, w_qkv, w_out, cotangent):
    n_row = lax.axis_size("row")
    n_col = lax.axis_size("colxdept")
    n_dp = lax.axis_size("dp")
    chips = n_col // 2
    tile = tokens.shape[1]
    seq = tile * n_col
    half, local = seq // 2, seq // n_row
    core = lax.axis_index("colxdept") % 2
    row = lax.axis_index("row").astype(jnp.int32)
    at = row[None]
    same_core = [list(range(c, n_col, 2)) for c in range(2)]

    def swap_cores(x):
        return lax.ppermute(x, "colxdept", [(i, i ^ 1) for i in range(n_col)])

    def swap_dp(x):
        return lax.ppermute(x, "dp", [(i, (i + 1) % n_dp) for i in range(n_dp)])

    def along_row(x, step):
        return lax.ppermute(x, "row", [(i, (i + step) % n_row) for i in range(n_row)])

    def among_chips(x):
        return lax.all_to_all(x, "colxdept", 0, 0, axis_index_groups=same_core)

    def gather_core(x, *others):
        copies = jnp.broadcast_to(x[None], (chips, *x.shape))
        return among_chips(after(copies, *others) if others else copies).reshape(half, -1)

    def gather_row(x):
        return [x] + [along_row(x, -j) for j in range(1, n_row)]

    def to_row(parts):
        return [parts[0]] + [along_row(parts[j], j) for j in range(1, n_row)]

    def total(parts):
        return sum(parts[1:], parts[0]).astype(BF16)

    index = jnp.arange(seq, dtype=jnp.int32)
    owner = (index // half + core) % 2
    position = ((index % half) // tile * 2 + owner) * tile + index % tile
    rows, cols = position[:, None], position[None, :]

    w_out_sib = swap_cores(w_out)
    w_qkv_sib = swap_cores(w_qkv)
    tok_mine, w_out_sib, w_qkv_sib = lax.optimization_barrier((gather_core(tokens[0]), w_out_sib, w_qkv_sib))
    tok_sib = swap_cores(tok_mine)
    other = swap_dp(after(jnp.concatenate([tokens[0], cotangent[0]], axis=1), tok_mine))
    qkv_parts = project(at, tok_mine, tok_sib, w_qkv, n_row)
    cot_mine = gather_core(cotangent[0], other, *qkv_parts)
    other_mine = gather_core(other, cot_mine)
    qkv_sum = total(to_row(qkv_parts))
    pieces = gather_row(qkv_sum)
    cot_mine = after(cot_mine, qkv_sum)
    cot_sib = after(swap_cores(cot_mine), pieces[1], pieces[3])
    back_parts = back_context(at, cot_mine, cot_sib, w_out, n_row)
    back_pieces = gather_row(total(to_row(back_parts)))
    back_pieces[0] = after(back_pieces[0], other_mine)

    done, second, quarter = attention(at, rows, cols, place(at, pieces, back_pieces), n_row)
    quarter = swap_dp(quarter)
    done_sib = swap_cores(second)
    mix_part = after(mix(chips, done, done_sib, w_out, w_out_sib), other_mine, quarter)
    mix_shares = among_chips(mix_part)
    other_sib = swap_cores(after(other_mine, mix_part))
    done2 = gather_row(quarter)
    back_part = back_tokens(chips, done, after(done_sib, mix_part, quarter), w_qkv, w_qkv_sib)
    mixed = jnp.sum(after(mix_shares, back_part, *done2).astype(F32), axis=0).astype(BF16)
    back_shares = among_chips(after(back_part, mixed))
    grad_out = weight_out(at, cot_mine, cot_sib, other_mine, other_sib, done, done2)
    grad_qkv = weight_qkv(at, tok_mine, tok_sib, other_mine, other_sib, done, done2)
    back_shares = after(back_shares, grad_out, grad_qkv)
    grad_tokens = jnp.sum(back_shares.astype(F32), axis=0).astype(BF16)
    return (mixed[None], grad_tokens[None], grad_qkv, grad_out)


def solution(mesh):
    return jax.shard_map(
        body,
        mesh=mesh,
        in_specs=(
            P("dp", "colxdept", "row"),
            P(None, "row", "colxdept"),
            P("colxdept", "row"),
            P("dp", "colxdept", "row"),
        ),
        out_specs=(
            P("dp", "colxdept", "row"),
            P("dp", "colxdept", "row"),
            P(None, "row", "colxdept"),
            P("colxdept", "row"),
        ),
        check_vma=False,
    )
```

```python
import jax
import jax.numpy as jnp
from jax import lax
from jax.experimental import pallas as pl
from jax.experimental.pallas import tpu as pltpu
from jax.sharding import PartitionSpec as P

DH = 128
F32 = jnp.float32
BF16 = jnp.bfloat16
NT = (((1,), (1,)), ((), ()))
TN = (((0,), (0,)), ((), ()))
ROOM = 56 * 2**20


def dot(a, b, dims=None):
    if dims is None:
        return jnp.dot(a, b, preferred_element_type=F32)
    return lax.dot_general(a, b, dims, preferred_element_type=F32)


def call(kernel, grid, in_specs, out_specs, out_shape, flops, scratch=()):
    def run(*args):
        many = out_shape if isinstance(out_shape, list) else [out_shape]
        moved = sum(a.size * a.dtype.itemsize for a in [*args, *many])
        return pl.pallas_call(
            kernel,
            grid=grid,
            in_specs=in_specs,
            out_specs=out_specs,
            out_shape=out_shape,
            scratch_shapes=list(scratch),
            compiler_params=pltpu.CompilerParams(vmem_limit_bytes=ROOM),
            cost_estimate=pl.CostEstimate(flops=flops, bytes_accessed=moved, transcendentals=0),
        )(*args)

    return run


def spec(block, index):
    return pl.BlockSpec(block, index)


def whole(x):
    return pl.BlockSpec(x.shape, lambda *_: (0,) * x.ndim)


SCALAR = pl.BlockSpec(memory_space=pltpu.SMEM)


def nth_part(row, j, n, part):
    return pl.ds(pl.multiple_of((row[0] + j) % n * part, part), part)


def project(row, mine, sib, w, n_row):
    n, depth, width = w.shape
    half = mine.shape[0]
    part = 2 * half // n_row

    def kernel(row, mine, sib, w, *rest):
        outs, held = rest[:-1], rest[-1]

        @pl.when(pl.program_id(0) == 0)
        def _():
            held[:half] = mine[...]
            held[half:] = sib[...]

        for j, out in enumerate(outs):
            out[...] = dot(held[nth_part(row, j, n_row, part)], w[...])

    return call(
        kernel,
        (n,),
        [SCALAR, whole(mine), whole(sib), spec((None, depth, width), lambda a: (a, 0, 0))],
        [spec((part, width), lambda a: (0, a))] * n_row,
        [jax.ShapeDtypeStruct((part, n * width), F32)] * n_row,
        4 * half * n * depth * width,
        [pltpu.VMEM((2 * half, depth), BF16)],
    )(row, mine, sib, w)


def back_half(x, w):
    width, depth = w.shape
    half = x.shape[0]
    step = min(1024, depth)

    def kernel(x, w, out):
        @pl.when(pl.program_id(0) == 0)
        def _():
            out[...] = jnp.zeros_like(out)

        out[...] += dot(x[...], w[...], NT)

    return call(
        kernel,
        (depth // step,),
        [spec((half, step), lambda k: (0, k)), spec((width, step), lambda k: (0, k))],
        spec((half, width), lambda k: (0, 0)),
        jax.ShapeDtypeStruct((half, width), F32),
        2 * half * depth * width,
    )(x, w)


def back_context(row, mine, sib, w, n_row):
    width, depth = w.shape
    half = sib.shape[0]
    part = 2 * half // n_row
    step = min(1024, depth)

    def kernel(row, mine, sib, w, *rest):
        outs, total = rest[:-1], rest[-1]

        @pl.when(pl.program_id(0) == 0)
        def _():
            total[:half] = mine[...]
            total[half:] = jnp.zeros_like(mine)

        total[half:] += dot(sib[...], w[...], NT)

        @pl.when(pl.program_id(0) == pl.num_programs(0) - 1)
        def _():
            for j, out in enumerate(outs):
                out[...] = total[nth_part(row, j, n_row, part)]

    return call(
        kernel,
        (depth // step,),
        [
            SCALAR,
            whole(mine),
            spec((half, step), lambda k: (0, k)),
            spec((width, step), lambda k: (0, k)),
        ],
        [spec((part, width), lambda k: (0, 0))] * n_row,
        [jax.ShapeDtypeStruct((part, width), F32)] * n_row,
        2 * half * depth * width,
        [pltpu.VMEM((2 * half, width), F32)],
    )(row, mine, sib, w)


def attention(row, rows, cols, pieces, back_pieces):
    n = len(pieces)
    part, width = back_pieces[0].shape
    seq = n * part
    half, heads = seq // 2, width // DH
    scale = 1.0 / DH**0.5

    def kernel(row, rows, cols, *rest):
        parts, (out, out_sib, out_part, held) = rest[: 2 * n], rest[2 * n :]

        @pl.when(pl.program_id(0) == 0)
        def _():
            for j in range(n):
                held[nth_part(row, j, n, part), : 3 * width] = parts[j][...]
                held[nth_part(row, j, n, part), 3 * width :] = parts[n + j][...]

        h = pl.program_id(0)
        q, k, v, g = [held[:, pl.ds(pl.multiple_of((a * heads + h) * DH, DH), DH)] for a in range(4)]
        scores = dot(q, k, NT) * scale
        scores = jnp.where(rows[...] >= cols[...], scores, -1e30)
        expo = jnp.exp(scores - jnp.max(scores, axis=-1, keepdims=True))
        probs = expo / jnp.sum(expo, axis=-1, keepdims=True)
        probs_b = probs.astype(BF16)
        out[0] = dot(probs_b, v).astype(BF16)
        out[3] = dot(probs_b, g, TN).astype(BF16)
        grad_probs = dot(g, v, NT)
        delta = jnp.sum(grad_probs * probs, axis=-1, keepdims=True)
        grad_scores = (probs * (grad_probs - delta) * scale).astype(BF16)
        out[1] = dot(grad_scores, k).astype(BF16)
        out[2] = dot(grad_scores, q, TN).astype(BF16)
        out_sib[...] = out[:, half:]
        out_part[...] = out[:, nth_part(row, 0, n, part)]

    return call(
        kernel,
        (heads,),
        [SCALAR, whole(rows), whole(cols)] + [whole(x) for x in (*pieces, *back_pieces)],
        [spec((4, r, DH), lambda h: (0, 0, h)) for r in (seq, half, part)],
        [jax.ShapeDtypeStruct((4, r, width), BF16) for r in (seq, half, part)],
        14 * heads * seq * seq * DH,
        [pltpu.VMEM((seq, 4 * width), BF16)],
    )(row, rows, cols, *pieces, *back_pieces)


def mix(chips, context, context_sib, w, w_sib):
    width, depth = w.shape
    half = context_sib.shape[1]
    step = min(1024, depth)

    def kernel(c, cs, w, ws, out):
        out[...] = (dot(c[...], w[...]) + dot(cs[...], ws[...])).astype(BF16).reshape(out.shape)

    c_spec = spec((None, half, width), lambda m: (0, 0, 0))
    w_spec = spec((width, step), lambda m: (0, m))
    return call(
        kernel,
        (depth // step,),
        [c_spec, c_spec, w_spec, w_spec],
        spec((chips, half // chips, step), lambda m: (0, 0, m)),
        jax.ShapeDtypeStruct((chips, half // chips, depth), BF16),
        4 * half * depth * width,
    )(context, context_sib, w, w_sib)


def back_tokens(chips, grads, grads_sib, w, w_sib):
    n, depth, width = w.shape
    half = grads_sib.shape[1]
    step = min(512, depth)

    def kernel(g, gs, w, ws, out):
        grads = jnp.concatenate([x[a + 1] for x in (g, gs) for a in range(n)], axis=1)
        weights = jnp.concatenate([x[a] for x in (w, ws) for a in range(n)], axis=1)
        out[...] = dot(grads, weights, NT).astype(BF16).reshape(out.shape)

    g_spec = spec((n + 1, half, width), lambda m: (0, 0, 0))
    w_spec = spec((n, step, width), lambda m: (0, m, 0))
    return call(
        kernel,
        (depth // step,),
        [g_spec, g_spec, w_spec, w_spec],
        spec((chips, half // chips, step), lambda m: (0, 0, m)),
        jax.ShapeDtypeStruct((chips, half // chips, depth), BF16),
        4 * half * n * depth * width,
    )(grads, grads_sib, w, w_sib)


def weight_qkv(row, mine, sib, other_mine, other_sib, done, done2):
    n, seq, width = done.shape[0] - 1, *done.shape[1:]
    half, depth = mine.shape
    pieces, part = len(done2), done2[0].shape[1]
    step = min(1024, depth)

    def kernel(row, t0, t1, t2, t3, d, *rest):
        d2, out, held = rest[:pieces], rest[-2], rest[-1]

        @pl.when(pl.program_id(0) == 0)
        def _():
            for a in range(n):
                columns = slice(a * width, (a + 1) * width)
                held[0, :, columns] = d[a + 1]
                for j in range(pieces):
                    held[1, nth_part(row, j, pieces, part), columns] = d2[j][a + 1]

        x = jnp.concatenate([t0[...], t1[...], t2[...], t3[...]], axis=0)
        total = dot(x, held[...].reshape(2 * seq, n * width), TN)
        for a in range(n):
            out[a] = total[:, a * width : (a + 1) * width].astype(BF16)

    t_spec = spec((half, step), lambda m: (0, m))
    return call(
        kernel,
        (depth // step,),
        [SCALAR] + [t_spec] * 4 + [whole(done)] + [whole(x) for x in done2],
        spec((n, step, width), lambda m: (0, m, 0)),
        jax.ShapeDtypeStruct((n, depth, width), BF16),
        4 * seq * n * depth * width,
        [pltpu.VMEM((2, seq, n * width), BF16)],
    )(row, mine, sib, other_mine, other_sib, done, *done2)


def weight_out(row, mine, sib, other_mine, other_sib, done, done2):
    seq, width = done.shape[1:]
    half, depth = mine.shape
    pieces, part = len(done2), done2[0].shape[1]
    step = min(1024, depth)
    first = depth // step

    def kernel(row, t0, t1, t2, t3, c, *rest):
        c2, out, held = rest[:pieces], rest[-2], rest[-1]

        @pl.when(pl.program_id(0) == 0)
        def _():
            held[0] = c[...].T
            for j in range(pieces):
                held[1, :, nth_part(row, j, pieces, part)] = c2[j][...].T

        total = dot(held[0], jnp.concatenate([t0[...], t1[...]], axis=0))
        total = total + dot(held[1], jnp.concatenate([t2[...], t3[...]], axis=0))
        out[...] = total.astype(BF16)

    t_spec = spec((half, step), lambda m: (0, m))
    o_spec = spec((half, step), lambda m: (0, first + m))
    return call(
        kernel,
        (depth // step,),
        [SCALAR, t_spec, t_spec, o_spec, o_spec, spec((None, seq, width), lambda m: (0, 0, 0))]
        + [spec((None, part, width), lambda m: (0, 0, 0))] * pieces,
        spec((width, step), lambda m: (0, m)),
        jax.ShapeDtypeStruct((width, depth), BF16),
        4 * seq * depth * width,
        [pltpu.VMEM((2, width, seq), BF16)],
    )(row, mine, sib, other_mine, other_sib, done, *done2)


def after(x, *others):
    return lax.optimization_barrier((x, *others))[0]


def body(tokens, w_qkv, w_out, cotangent):
    n_row = lax.axis_size("row")
    n_col = lax.axis_size("colxdept")
    n_dp = lax.axis_size("dp")
    chips = n_col // 2
    tile = tokens.shape[1]
    seq = tile * n_col
    half, local = seq // 2, seq // n_row
    core = lax.axis_index("colxdept") % 2
    row = lax.axis_index("row").astype(jnp.int32)
    at = row[None]
    same_core = [list(range(c, n_col, 2)) for c in range(2)]

    def swap_cores(x):
        return lax.ppermute(x, "colxdept", [(i, i ^ 1) for i in range(n_col)])

    def swap_dp(x):
        return lax.ppermute(x, "dp", [(i, (i + 1) % n_dp) for i in range(n_dp)])

    def along_row(x, step):
        return lax.ppermute(x, "row", [(i, (i + step) % n_row) for i in range(n_row)])

    def among_chips(x):
        return lax.all_to_all(x, "colxdept", 0, 0, axis_index_groups=same_core)

    def gather_core(x, *others):
        copies = jnp.broadcast_to(x[None], (chips, *x.shape))
        return among_chips(after(copies, *others) if others else copies).reshape(half, -1)

    def gather_row(x):
        return [x] + [along_row(x, -j) for j in range(1, n_row)]

    def to_row(parts):
        return [parts[0]] + [along_row(parts[j], j) for j in range(1, n_row)]

    def total(parts):
        return sum(parts[1:], parts[0]).astype(BF16)

    index = jnp.arange(seq, dtype=jnp.int32)
    owner = (index // half + core) % 2
    position = ((index % half) // tile * 2 + owner) * tile + index % tile
    rows, cols = position[:, None], position[None, :]

    w_out_sib = swap_cores(w_out)
    w_qkv_sib = swap_cores(w_qkv)
    tok_mine, w_out_sib, w_qkv_sib = lax.optimization_barrier((gather_core(tokens[0]), w_out_sib, w_qkv_sib))
    tok_sib = swap_cores(tok_mine)
    other = swap_dp(after(jnp.concatenate([tokens[0], cotangent[0]], axis=1), tok_mine))
    qkv_parts = project(at, tok_mine, tok_sib, w_qkv, n_row)
    cot_mine = gather_core(cotangent[0], other, *qkv_parts)
    other_mine = gather_core(other, cot_mine)
    qkv_sum = total(to_row(qkv_parts))
    pieces = gather_row(qkv_sum)
    cot_mine = after(cot_mine, qkv_sum)
    cot_sib = after(swap_cores(cot_mine), pieces[1], pieces[3])
    back_parts = back_context(at, back_half(cot_mine, w_out), cot_sib, w_out, n_row)
    back_pieces = gather_row(total(to_row(back_parts)))
    back_pieces[0] = after(back_pieces[0], other_mine)

    done, second, quarter = attention(at, rows, cols, pieces, back_pieces)
    quarter = swap_dp(quarter)
    done_sib = swap_cores(second)
    mix_part = after(mix(chips, done, done_sib, w_out, w_out_sib), other_mine, quarter)
    mix_shares = among_chips(mix_part)
    other_sib = swap_cores(after(other_mine, mix_part))
    done2 = gather_row(quarter)
    back_part = back_tokens(chips, done, after(done_sib, mix_part, quarter), w_qkv, w_qkv_sib)
    mixed = jnp.sum(after(mix_shares, back_part, *done2).astype(F32), axis=0).astype(BF16)
    back_shares = among_chips(after(back_part, mixed))
    grad_out = weight_out(at, cot_mine, cot_sib, other_mine, other_sib, done, done2)
    grad_qkv = weight_qkv(at, tok_mine, tok_sib, other_mine, other_sib, done, done2)
    back_shares = after(back_shares, grad_out, grad_qkv)
    grad_tokens = jnp.sum(back_shares.astype(F32), axis=0).astype(BF16)
    return (mixed[None], grad_tokens[None], grad_qkv, grad_out)


def solution(mesh):
    return jax.shard_map(
        body,
        mesh=mesh,
        in_specs=(
            P("dp", "colxdept", "row"),
            P(None, "row", "colxdept"),
            P("colxdept", "row"),
            P("dp", "colxdept", "row"),
        ),
        out_specs=(
            P("dp", "colxdept", "row"),
            P("dp", "colxdept", "row"),
            P(None, "row", "colxdept"),
            P("colxdept", "row"),
        ),
        check_vma=False,
    )
```

```python
import jax
import jax.numpy as jnp
from jax import lax
from jax.experimental import pallas as pl
from jax.experimental.pallas import tpu as pltpu
from jax.sharding import PartitionSpec as P

DH = 128
F32 = jnp.float32
BF16 = jnp.bfloat16
NT = (((1,), (1,)), ((), ()))
TN = (((0,), (0,)), ((), ()))
ROOM = 56 * 2**20


def dot(a, b, dims=None):
    if dims is None:
        return jnp.dot(a, b, preferred_element_type=F32)
    return lax.dot_general(a, b, dims, preferred_element_type=F32)


def call(kernel, grid, in_specs, out_specs, out_shape, flops, scratch=(), aliases=None):
    def run(*args):
        many = out_shape if isinstance(out_shape, list) else [out_shape]
        moved = sum(a.size * a.dtype.itemsize for a in [*args, *many])
        return pl.pallas_call(
            kernel,
            grid=grid,
            in_specs=in_specs,
            out_specs=out_specs,
            out_shape=out_shape,
            scratch_shapes=list(scratch),
            input_output_aliases=aliases or {},
            compiler_params=pltpu.CompilerParams(vmem_limit_bytes=ROOM),
            cost_estimate=pl.CostEstimate(flops=flops, bytes_accessed=moved, transcendentals=0),
        )(*args)

    return run


def spec(block, index):
    return pl.BlockSpec(block, index)


def whole(x):
    return pl.BlockSpec(x.shape, lambda *_: (0,) * x.ndim)


SCALAR = pl.BlockSpec(memory_space=pltpu.SMEM)


def nth_part(row, j, n, part):
    return pl.ds(pl.multiple_of((row[0] + j) % n * part, part), part)


def project(row, mine, sib, w, n_row):
    n, depth, width = w.shape
    half = mine.shape[0]
    part = 2 * half // n_row

    def kernel(row, mine, sib, w, *rest):
        outs, held = rest[:-1], rest[-1]

        @pl.when(pl.program_id(0) == 0)
        def _():
            held[:half] = mine[...]
            held[half:] = sib[...]

        for j, out in enumerate(outs):
            out[...] = dot(held[nth_part(row, j, n_row, part)], w[...])

    return call(
        kernel,
        (n,),
        [SCALAR, whole(mine), whole(sib), spec((None, depth, width), lambda a: (a, 0, 0))],
        [spec((part, width), lambda a: (0, a))] * n_row,
        [jax.ShapeDtypeStruct((part, n * width), F32)] * n_row,
        4 * half * n * depth * width,
        [pltpu.VMEM((2 * half, depth), BF16)],
    )(row, mine, sib, w)


def back_half(x, w):
    width, depth = w.shape
    half = x.shape[0]
    step = min(1024, depth)

    def kernel(x, w, out):
        @pl.when(pl.program_id(0) == 0)
        def _():
            out[...] = jnp.zeros_like(out)

        out[...] += dot(x[...], w[...], NT)

    return call(
        kernel,
        (depth // step,),
        [spec((half, step), lambda k: (0, k)), spec((width, step), lambda k: (0, k))],
        spec((half, width), lambda k: (0, 0)),
        jax.ShapeDtypeStruct((half, width), F32),
        2 * half * depth * width,
    )(x, w)


def back_context(row, mine, sib, w, n_row):
    width, depth = w.shape
    half = sib.shape[0]
    part = 2 * half // n_row
    step = min(1024, depth)

    def kernel(row, mine, sib, w, *rest):
        outs, total = rest[:-1], rest[-1]

        @pl.when(pl.program_id(0) == 0)
        def _():
            total[:half] = mine[...]
            total[half:] = jnp.zeros_like(mine)

        total[half:] += dot(sib[...], w[...], NT)

        @pl.when(pl.program_id(0) == pl.num_programs(0) - 1)
        def _():
            for j, out in enumerate(outs):
                out[...] = total[nth_part(row, j, n_row, part)]

    return call(
        kernel,
        (depth // step,),
        [
            SCALAR,
            whole(mine),
            spec((half, step), lambda k: (0, k)),
            spec((width, step), lambda k: (0, k)),
        ],
        [spec((part, width), lambda k: (0, 0))] * n_row,
        [jax.ShapeDtypeStruct((part, width), F32)] * n_row,
        2 * half * depth * width,
        [pltpu.VMEM((2 * half, width), F32)],
    )(row, mine, sib, w)


def attention(row, rows, cols, pieces, back_pieces):
    n = len(pieces)
    part, width = back_pieces[0].shape
    seq = n * part
    half, heads = seq // 2, width // DH
    scale = 1.0 / DH**0.5

    def kernel(row, rows, cols, *rest):
        parts, (out, out_sib, out_part, held) = rest[: 2 * n], rest[2 * n :]

        @pl.when(pl.program_id(0) == 0)
        def _():
            for j in range(n):
                held[nth_part(row, j, n, part), : 3 * width] = parts[j][...]
                held[nth_part(row, j, n, part), 3 * width :] = parts[n + j][...]

        h = pl.program_id(0)
        q, k, v, g = [held[:, pl.ds(pl.multiple_of((a * heads + h) * DH, DH), DH)] for a in range(4)]
        scores = dot(q, k, NT) * scale
        scores = jnp.where(rows[...] >= cols[...], scores, -1e30)
        expo = jnp.exp(scores - jnp.max(scores, axis=-1, keepdims=True))
        probs = expo / jnp.sum(expo, axis=-1, keepdims=True)
        probs_b = probs.astype(BF16)
        out[0] = dot(probs_b, v).astype(BF16)
        out[3] = dot(probs_b, g, TN).astype(BF16)
        grad_probs = dot(g, v, NT)
        delta = jnp.sum(grad_probs * probs, axis=-1, keepdims=True)
        grad_scores = (probs * (grad_probs - delta) * scale).astype(BF16)
        out[1] = dot(grad_scores, k).astype(BF16)
        out[2] = dot(grad_scores, q, TN).astype(BF16)
        out_sib[...] = out[:, half:]
        out_part[...] = out[:, nth_part(row, 0, n, part)]

    return call(
        kernel,
        (heads,),
        [SCALAR, whole(rows), whole(cols)] + [whole(x) for x in (*pieces, *back_pieces)],
        [spec((4, r, DH), lambda h: (0, 0, h)) for r in (seq, half, part)],
        [jax.ShapeDtypeStruct((4, r, width), BF16) for r in (seq, half, part)],
        14 * heads * seq * seq * DH,
        [pltpu.VMEM((seq, 4 * width), BF16)],
    )(row, rows, cols, *pieces, *back_pieces)


def mix(chips, done, done_sib, w, w_sib):
    width, depth = w.shape
    half = done_sib.shape[1]
    step = min(1024, depth)

    def kernel(d, ds, w, ws, out):
        out[...] = (dot(d[...], w[...]) + dot(ds[...], ws[...])).astype(BF16).reshape(out.shape)

    d_spec = spec((None, half, width), lambda m: (0, 0, 0))
    w_spec = spec((width, step), lambda m: (0, m))
    return call(
        kernel,
        (depth // step,),
        [d_spec, d_spec, w_spec, w_spec],
        spec((chips, None, half // chips, step), lambda m: (0, 0, 0, m)),
        jax.ShapeDtypeStruct((chips, 2, half // chips, depth), BF16),
        4 * half * depth * width,
    )(done, done_sib, w, w_sib)


def back_tokens(first, done, done_sib, w, w_sib):
    n, depth, width = w.shape
    chips, half = first.shape[0], done_sib.shape[1]
    step = min(512, depth)

    def side(x, start):
        return [x[a] for a in range(start, n + start)]

    def kernel(_, d, ds, w, ws, out):
        grads = jnp.concatenate(side(d, 1) + side(ds, 1), axis=1)
        weights = jnp.concatenate(side(w, 0) + side(ws, 0), axis=1)
        out[...] = dot(grads, weights, NT).astype(BF16).reshape(out.shape)

    d_spec = spec((n + 1, half, width), lambda m: (0, 0, 0))
    w_spec = spec((n, step, width), lambda m: (0, m, 0))
    return call(
        kernel,
        (depth // step,),
        [pl.BlockSpec(memory_space=pl.ANY), d_spec, d_spec, w_spec, w_spec],
        spec((chips, None, half // chips, step), lambda m: (0, 1, 0, m)),
        jax.ShapeDtypeStruct(first.shape, BF16),
        4 * half * n * depth * width,
        aliases={0: 0},
    )(first, done, done_sib, w, w_sib)


def weight_own(tok_mine, tok_sib, cot_mine, cot_sib, done):
    n, seq, width = done.shape[0] - 1, *done.shape[1:]
    half, depth = tok_mine.shape
    step = min(512, depth)

    def kernel(t0, t1, c0, c1, d, out_qkv, out_out, held):
        @pl.when(pl.program_id(0) == 0)
        def _():
            held[...] = d[0].T

        x = jnp.concatenate([t0[...], t1[...]], axis=0)
        for a in range(n):
            out_qkv[a] = dot(x, d[a + 1], TN)
        out_out[...] = dot(held[...], jnp.concatenate([c0[...], c1[...]], axis=0))

    x_spec = spec((half, step), lambda m: (0, m))
    return call(
        kernel,
        (depth // step,),
        [x_spec] * 4 + [whole(done)],
        [spec((n, step, width), lambda m: (0, m, 0)), spec((width, step), lambda m: (0, m))],
        [jax.ShapeDtypeStruct((n, depth, width), F32), jax.ShapeDtypeStruct((width, depth), F32)],
        2 * seq * (n + 1) * depth * width,
        [pltpu.VMEM((width, seq), BF16)],
    )(tok_mine, tok_sib, cot_mine, cot_sib, done)


def weight_both(row, own_qkv, own_out, mine, sib, pieces):
    n, depth, width = own_qkv.shape
    half = mine.shape[0]
    count, part = len(pieces), pieces[0].shape[1]
    seq = count * part
    step = min(512, depth)
    steps = depth // step

    def kernel(row, q, o, t0, t1, c0, c1, *rest):
        parts, (out_qkv, out_out, held, turned) = rest[:count], rest[count:]

        @pl.when(pl.program_id(0) == 0)
        def _():
            for j in range(count):
                rows = nth_part(row, j, count, part)
                held[:, rows] = parts[j][1:]
                turned[:, rows] = parts[j][0].T

        x = jnp.concatenate([t0[...], t1[...]], axis=0)
        for a in range(n):
            out_qkv[a] = (q[a] + dot(x, held[a], TN)).astype(BF16)
        y = jnp.concatenate([c0[...], c1[...]], axis=0)
        out_out[...] = (o[...] + dot(turned[...], y)).astype(BF16)

    t_spec = spec((half, step), lambda m: (0, m))
    c_spec = spec((half, step), lambda m: (0, steps + m))
    q_spec = spec((n, step, width), lambda m: (0, m, 0))
    o_spec = spec((width, step), lambda m: (0, m))
    return call(
        kernel,
        (steps,),
        [SCALAR, q_spec, o_spec, t_spec, t_spec, c_spec, c_spec] + [whole(x) for x in pieces],
        [q_spec, o_spec],
        [jax.ShapeDtypeStruct((n, depth, width), BF16), jax.ShapeDtypeStruct((width, depth), BF16)],
        2 * seq * (n + 1) * depth * width,
        [pltpu.VMEM((n, seq, width), BF16), pltpu.VMEM((width, seq), BF16)],
    )(row, own_qkv, own_out, mine, sib, mine, sib, *pieces)


def after(x, *others):
    return lax.optimization_barrier((x, *others))[0]


def body(tokens, w_qkv, w_out, cotangent):
    n_row = lax.axis_size("row")
    n_col = lax.axis_size("colxdept")
    n_dp = lax.axis_size("dp")
    chips = n_col // 2
    tile = tokens.shape[1]
    seq = tile * n_col
    half, local = seq // 2, seq // n_row
    core = lax.axis_index("colxdept") % 2
    row = lax.axis_index("row").astype(jnp.int32)
    at = row[None]
    same_core = [list(range(c, n_col, 2)) for c in range(2)]

    def swap_cores(x):
        return lax.ppermute(x, "colxdept", [(i, i ^ 1) for i in range(n_col)])

    def swap_dp(x):
        return lax.ppermute(x, "dp", [(i, (i + 1) % n_dp) for i in range(n_dp)])

    def along_row(x, step):
        return lax.ppermute(x, "row", [(i, (i + step) % n_row) for i in range(n_row)])

    def among_chips(x):
        return lax.all_to_all(x, "colxdept", 0, 0, axis_index_groups=same_core)

    def gather_core(x, *others):
        copies = jnp.broadcast_to(x[None], (chips, *x.shape))
        return among_chips(after(copies, *others) if others else copies).reshape(half, -1)

    def gather_row(x):
        return [x] + [along_row(x, -j) for j in range(1, n_row)]

    def to_row(parts):
        return [parts[0]] + [along_row(parts[j], j) for j in range(1, n_row)]

    def total(parts):
        return sum(parts[1:], parts[0]).astype(BF16)

    index = jnp.arange(seq, dtype=jnp.int32)
    owner = (index // half + core) % 2
    position = ((index % half) // tile * 2 + owner) * tile + index % tile
    rows, cols = position[:, None], position[None, :]

    w_out_sib = swap_cores(w_out)
    w_qkv_sib = swap_cores(w_qkv)
    tok_mine, w_out_sib, w_qkv_sib = lax.optimization_barrier((gather_core(tokens[0]), w_out_sib, w_qkv_sib))
    tok_sib = swap_cores(tok_mine)
    other = swap_dp(after(jnp.concatenate([tokens[0], cotangent[0]], axis=1), tok_mine))
    qkv_parts = project(at, tok_mine, tok_sib, w_qkv, n_row)
    cot_mine = gather_core(cotangent[0], other, *qkv_parts)
    other_mine = gather_core(other, cot_mine)
    qkv_sum = total(to_row(qkv_parts))
    pieces = gather_row(qkv_sum)
    cot_mine = after(cot_mine, qkv_sum)
    cot_sib = after(swap_cores(cot_mine), pieces[1], pieces[3])
    back_parts = back_context(at, back_half(cot_mine, w_out), cot_sib, w_out, n_row)
    back_pieces = gather_row(total(to_row(back_parts)))
    back_pieces[0] = after(back_pieces[0], other_mine)

    done, second, quarter = attention(at, rows, cols, pieces, back_pieces)
    quarter = swap_dp(quarter)
    done_sib = swap_cores(second)
    first = mix(chips, done, done_sib, w_out, w_out_sib)
    both = back_tokens(first, done, done_sib, w_qkv, w_qkv_sib)
    both, quarter, other_mine = lax.optimization_barrier((both, quarter, other_mine))
    done2 = gather_row(quarter)
    other_sib = swap_cores(other_mine)
    shares = among_chips(both)
    own_qkv, own_out = weight_own(tok_mine, tok_sib, cot_mine, cot_sib, after(done, both))
    grad_qkv, grad_out = weight_both(at, own_qkv, own_out, other_mine, other_sib, done2)
    shares = after(shares, grad_out, grad_qkv)
    results = jnp.sum(shares.astype(F32), axis=0).astype(BF16)
    return (results[:1], results[1:], grad_qkv, grad_out)


def solution(mesh):
    return jax.shard_map(
        body,
        mesh=mesh,
        in_specs=(
            P("dp", "colxdept", "row"),
            P(None, "row", "colxdept"),
            P("colxdept", "row"),
            P("dp", "colxdept", "row"),
        ),
        out_specs=(
            P("dp", "colxdept", "row"),
            P("dp", "colxdept", "row"),
            P(None, "row", "colxdept"),
            P("colxdept", "row"),
        ),
        check_vma=False,
    )
```

```python
import jax
import jax.numpy as jnp
from jax import lax
from jax.experimental import pallas as pl
from jax.experimental.pallas import tpu as pltpu
from jax.sharding import PartitionSpec as P

DH = 128
F32 = jnp.float32
BF16 = jnp.bfloat16
NT = (((1,), (1,)), ((), ()))
TN = (((0,), (0,)), ((), ()))
ROOM = 56 * 2**20


def dot(a, b, dims=None):
    if dims is None:
        return jnp.dot(a, b, preferred_element_type=F32)
    return lax.dot_general(a, b, dims, preferred_element_type=F32)


def call(kernel, grid, in_specs, out_specs, out_shape, flops, scratch=()):
    def run(*args):
        many = out_shape if isinstance(out_shape, list) else [out_shape]
        moved = sum(a.size * a.dtype.itemsize for a in [*args, *many])
        return pl.pallas_call(
            kernel,
            grid=grid,
            in_specs=in_specs,
            out_specs=out_specs,
            out_shape=out_shape,
            scratch_shapes=list(scratch),
            compiler_params=pltpu.CompilerParams(vmem_limit_bytes=ROOM),
            cost_estimate=pl.CostEstimate(flops=flops, bytes_accessed=moved, transcendentals=0),
        )(*args)

    return run


def spec(block, index):
    return pl.BlockSpec(block, index)


def whole(x):
    return pl.BlockSpec(x.shape, lambda *_: (0,) * x.ndim)


SCALAR = pl.BlockSpec(memory_space=pltpu.SMEM)


def nth_part(row, j, n, part):
    return pl.ds(pl.multiple_of((row[0] + j) % n * part, part), part)


def project(row, mine, sib, w, n_row):
    n, depth, width = w.shape
    half = mine.shape[0]
    part = 2 * half // n_row

    def kernel(row, mine, sib, w, *rest):
        outs, held = rest[:-1], rest[-1]

        @pl.when(pl.program_id(0) == 0)
        def _():
            held[:half] = mine[...]
            held[half:] = sib[...]

        for j, out in enumerate(outs):
            out[...] = dot(held[nth_part(row, j, n_row, part)], w[...])

    return call(
        kernel,
        (n,),
        [SCALAR, whole(mine), whole(sib), spec((None, depth, width), lambda a: (a, 0, 0))],
        [spec((part, width), lambda a: (0, a))] * n_row,
        [jax.ShapeDtypeStruct((part, n * width), F32)] * n_row,
        4 * half * n * depth * width,
        [pltpu.VMEM((2 * half, depth), BF16)],
    )(row, mine, sib, w)


def back_half(x, w):
    width, depth = w.shape
    half = x.shape[0]
    step = min(1024, depth)

    def kernel(x, w, out):
        @pl.when(pl.program_id(0) == 0)
        def _():
            out[...] = jnp.zeros_like(out)

        out[...] += dot(x[...], w[...], NT)

    return call(
        kernel,
        (depth // step,),
        [spec((half, step), lambda k: (0, k)), spec((width, step), lambda k: (0, k))],
        spec((half, width), lambda k: (0, 0)),
        jax.ShapeDtypeStruct((half, width), F32),
        2 * half * depth * width,
    )(x, w)


def back_context(row, mine, sib, w, n_row):
    width, depth = w.shape
    half = sib.shape[0]
    part = 2 * half // n_row
    step = min(1024, depth)

    def kernel(row, mine, sib, w, *rest):
        outs, total = rest[:-1], rest[-1]

        @pl.when(pl.program_id(0) == 0)
        def _():
            total[:half] = mine[...]
            total[half:] = jnp.zeros_like(mine)

        total[half:] += dot(sib[...], w[...], NT)

        @pl.when(pl.program_id(0) == pl.num_programs(0) - 1)
        def _():
            for j, out in enumerate(outs):
                out[...] = total[nth_part(row, j, n_row, part)]

    return call(
        kernel,
        (depth // step,),
        [
            SCALAR,
            whole(mine),
            spec((half, step), lambda k: (0, k)),
            spec((width, step), lambda k: (0, k)),
        ],
        [spec((part, width), lambda k: (0, 0))] * n_row,
        [jax.ShapeDtypeStruct((part, width), F32)] * n_row,
        2 * half * depth * width,
        [pltpu.VMEM((2 * half, width), F32)],
    )(row, mine, sib, w)


def attention(row, rows, cols, pieces, back_pieces):
    n = len(pieces)
    part, width = back_pieces[0].shape
    seq = n * part
    half, heads = seq // 2, width // DH
    scale = 1.0 / DH**0.5

    def kernel(row, rows, cols, *rest):
        parts, (out, out_sib, out_part, held) = rest[: 2 * n], rest[2 * n :]

        @pl.when(pl.program_id(0) == 0)
        def _():
            for j in range(n):
                held[nth_part(row, j, n, part), : 3 * width] = parts[j][...]
                held[nth_part(row, j, n, part), 3 * width :] = parts[n + j][...]

        h = pl.program_id(0)
        q, k, v, g = [held[:, pl.ds(pl.multiple_of((a * heads + h) * DH, DH), DH)] for a in range(4)]
        scores = dot(q, k, NT) * scale
        scores = jnp.where(rows[...] >= cols[...], scores, -1e30)
        expo = jnp.exp(scores - jnp.max(scores, axis=-1, keepdims=True))
        probs = expo / jnp.sum(expo, axis=-1, keepdims=True)
        probs_b = probs.astype(BF16)
        out[0] = dot(probs_b, v).astype(BF16)
        out[3] = dot(probs_b, g, TN).astype(BF16)
        grad_probs = dot(g, v, NT)
        delta = jnp.sum(grad_probs * probs, axis=-1, keepdims=True)
        grad_scores = (probs * (grad_probs - delta) * scale).astype(BF16)
        out[1] = dot(grad_scores, k).astype(BF16)
        out[2] = dot(grad_scores, q, TN).astype(BF16)
        out_sib[...] = out[:, half:]
        out_part[...] = out[:, nth_part(row, 0, n, part)]

    return call(
        kernel,
        (heads,),
        [SCALAR, whole(rows), whole(cols)] + [whole(x) for x in (*pieces, *back_pieces)],
        [spec((4, r, DH), lambda h: (0, 0, h)) for r in (seq, half, part)],
        [jax.ShapeDtypeStruct((4, r, width), BF16) for r in (seq, half, part)],
        14 * heads * seq * seq * DH,
        [pltpu.VMEM((seq, 4 * width), BF16)],
    )(row, rows, cols, *pieces, *back_pieces)


def partials(chips, done, done_sib, w_out, w_out_sib, w_qkv, w_qkv_sib):
    n, depth, width = w_qkv.shape
    half = done_sib.shape[1]
    step = min(512, depth)

    def side(x, first):
        return jnp.concatenate([x[a] for a in range(first, n + first)], axis=1)

    def kernel(d, ds, wo, wos, wq, wqs, out):
        mixed = dot(d[0], wo[...]) + dot(ds[0], wos[...])
        out[:, 0] = mixed.astype(BF16).reshape(out.shape[0], *out.shape[2:])
        grads = jnp.concatenate([side(d, 1), side(ds, 1)], axis=1)
        weights = jnp.concatenate([side(wq, 0), side(wqs, 0)], axis=1)
        out[:, 1] = dot(grads, weights, NT).astype(BF16).reshape(out.shape[0], *out.shape[2:])

    d_spec = spec((n + 1, half, width), lambda m: (0, 0, 0))
    o_spec = spec((width, step), lambda m: (0, m))
    q_spec = spec((n, step, width), lambda m: (0, m, 0))
    return call(
        kernel,
        (depth // step,),
        [d_spec, d_spec, o_spec, o_spec, q_spec, q_spec],
        spec((chips, 2, half // chips, step), lambda m: (0, 0, 0, m)),
        jax.ShapeDtypeStruct((chips, 2, half // chips, depth), BF16),
        4 * half * (n + 1) * depth * width,
    )(done, done_sib, w_out, w_out_sib, w_qkv, w_qkv_sib)


def weight_own(tok_mine, tok_sib, cot_mine, cot_sib, done):
    n, seq, width = done.shape[0] - 1, *done.shape[1:]
    half, depth = tok_mine.shape
    step = min(512, depth)

    def kernel(t0, t1, c0, c1, d, out_qkv, out_out, held):
        @pl.when(pl.program_id(0) == 0)
        def _():
            held[...] = d[0].T

        x = jnp.concatenate([t0[...], t1[...]], axis=0)
        for a in range(n):
            out_qkv[a] = dot(x, d[a + 1], TN)
        out_out[...] = dot(held[...], jnp.concatenate([c0[...], c1[...]], axis=0))

    x_spec = spec((half, step), lambda m: (0, m))
    return call(
        kernel,
        (depth // step,),
        [x_spec] * 4 + [whole(done)],
        [spec((n, step, width), lambda m: (0, m, 0)), spec((width, step), lambda m: (0, m))],
        [jax.ShapeDtypeStruct((n, depth, width), F32), jax.ShapeDtypeStruct((width, depth), F32)],
        2 * seq * (n + 1) * depth * width,
        [pltpu.VMEM((width, seq), BF16)],
    )(tok_mine, tok_sib, cot_mine, cot_sib, done)


def weight_both(row, own_qkv, own_out, mine, sib, pieces):
    n, depth, width = own_qkv.shape
    half = mine.shape[0]
    count, part = len(pieces), pieces[0].shape[1]
    seq = count * part
    step = min(512, depth)
    steps = depth // step

    def kernel(row, q, o, t0, t1, c0, c1, *rest):
        parts, (out_qkv, out_out, held, turned) = rest[:count], rest[count:]

        @pl.when(pl.program_id(0) == 0)
        def _():
            for j in range(count):
                rows = nth_part(row, j, count, part)
                held[:, rows] = parts[j][1:]
                turned[:, rows] = parts[j][0].T

        x = jnp.concatenate([t0[...], t1[...]], axis=0)
        for a in range(n):
            out_qkv[a] = (q[a] + dot(x, held[a], TN)).astype(BF16)
        y = jnp.concatenate([c0[...], c1[...]], axis=0)
        out_out[...] = (o[...] + dot(turned[...], y)).astype(BF16)

    t_spec = spec((half, step), lambda m: (0, m))
    c_spec = spec((half, step), lambda m: (0, steps + m))
    q_spec = spec((n, step, width), lambda m: (0, m, 0))
    o_spec = spec((width, step), lambda m: (0, m))
    return call(
        kernel,
        (steps,),
        [SCALAR, q_spec, o_spec, t_spec, t_spec, c_spec, c_spec] + [whole(x) for x in pieces],
        [q_spec, o_spec],
        [jax.ShapeDtypeStruct((n, depth, width), BF16), jax.ShapeDtypeStruct((width, depth), BF16)],
        2 * seq * (n + 1) * depth * width,
        [pltpu.VMEM((n, seq, width), BF16), pltpu.VMEM((width, seq), BF16)],
    )(row, own_qkv, own_out, mine, sib, mine, sib, *pieces)


def after(x, *others):
    return lax.optimization_barrier((x, *others))[0]


def body(tokens, w_qkv, w_out, cotangent):
    n_row = lax.axis_size("row")
    n_col = lax.axis_size("colxdept")
    n_dp = lax.axis_size("dp")
    chips = n_col // 2
    tile = tokens.shape[1]
    seq = tile * n_col
    half, local = seq // 2, seq // n_row
    core = lax.axis_index("colxdept") % 2
    row = lax.axis_index("row").astype(jnp.int32)
    at = row[None]
    same_core = [list(range(c, n_col, 2)) for c in range(2)]

    def swap_cores(x):
        return lax.ppermute(x, "colxdept", [(i, i ^ 1) for i in range(n_col)])

    def swap_dp(x):
        return lax.ppermute(x, "dp", [(i, (i + 1) % n_dp) for i in range(n_dp)])

    def along_row(x, step):
        return lax.ppermute(x, "row", [(i, (i + step) % n_row) for i in range(n_row)])

    def among_chips(x):
        return lax.all_to_all(x, "colxdept", 0, 0, axis_index_groups=same_core)

    def gather_core(x, *others):
        copies = jnp.broadcast_to(x[None], (chips, *x.shape))
        return among_chips(after(copies, *others) if others else copies).reshape(half, -1)

    def gather_row(x):
        return [x] + [along_row(x, -j) for j in range(1, n_row)]

    def to_row(parts):
        return [parts[0]] + [along_row(parts[j], j) for j in range(1, n_row)]

    def total(parts):
        return sum(parts[1:], parts[0]).astype(BF16)

    index = jnp.arange(seq, dtype=jnp.int32)
    owner = (index // half + core) % 2
    position = ((index % half) // tile * 2 + owner) * tile + index % tile
    rows, cols = position[:, None], position[None, :]

    w_out_sib = swap_cores(w_out)
    w_qkv_sib = swap_cores(w_qkv)
    tok_mine, w_out_sib, w_qkv_sib = lax.optimization_barrier((gather_core(tokens[0]), w_out_sib, w_qkv_sib))
    tok_sib = swap_cores(tok_mine)
    other = swap_dp(after(jnp.concatenate([tokens[0], cotangent[0]], axis=1), tok_mine))
    qkv_parts = project(at, tok_mine, tok_sib, w_qkv, n_row)
    cot_mine = gather_core(cotangent[0], other, *qkv_parts)
    other_mine = gather_core(other, cot_mine)
    qkv_sum = total(to_row(qkv_parts))
    pieces = gather_row(qkv_sum)
    cot_mine = after(cot_mine, qkv_sum)
    cot_sib = after(swap_cores(cot_mine), pieces[1], pieces[3])
    back_parts = back_context(at, back_half(cot_mine, w_out), cot_sib, w_out, n_row)
    back_pieces = gather_row(total(to_row(back_parts)))
    back_pieces[0] = after(back_pieces[0], other_mine)

    done, second, quarter = attention(at, rows, cols, pieces, back_pieces)
    quarter = swap_dp(quarter)
    done_sib = swap_cores(second)
    both = partials(chips, done, done_sib, w_out, w_out_sib, w_qkv, w_qkv_sib)
    both, quarter, other_mine = lax.optimization_barrier((both, quarter, other_mine))
    done2 = gather_row(quarter)
    other_sib = swap_cores(other_mine)
    shares = among_chips(both)
    own_qkv, own_out = weight_own(tok_mine, tok_sib, cot_mine, cot_sib, after(done, both))
    grad_qkv, grad_out = weight_both(at, own_qkv, own_out, other_mine, other_sib, done2)
    shares = after(shares, grad_out, grad_qkv)
    mixed, grad_tokens = [jnp.sum(shares[:, a].astype(F32), axis=0).astype(BF16) for a in range(2)]
    return (mixed[None], grad_tokens[None], grad_qkv, grad_out)


def solution(mesh):
    return jax.shard_map(
        body,
        mesh=mesh,
        in_specs=(
            P("dp", "colxdept", "row"),
            P(None, "row", "colxdept"),
            P("colxdept", "row"),
            P("dp", "colxdept", "row"),
        ),
        out_specs=(
            P("dp", "colxdept", "row"),
            P("dp", "colxdept", "row"),
            P(None, "row", "colxdept"),
            P("colxdept", "row"),
        ),
        check_vma=False,
    )
```
